32 devices in a mesh: groups: 2 (over y), wide: 16 (over z, x, core).
Axes of the slice: x: 2, y: 2, z: 4, core: 2. Of those that a mesh axis runs over, the one named last changes fastest.
Arguments:
- features: bfloat16 [4096, 8192], P(('groups', 'wide')), parts along dimension 0, may hold values from -6 to 6
- cotangent: bfloat16 [4096, 1024], P(('groups', 'wide')), parts along dimension 0, may hold values from -6 to 6
- frozen_key_weight: bfloat16 [8192, 1024], P('wide'), may hold values from -0.0625 to 0.0625
- adapter_down_weight: bfloat16 [32, 8192, 64], P(('groups', 'wide')), parts along dimension 0, may hold values from -0.0625 to 0.0625
- adapter_up_weight: bfloat16 [32, 64, 1024], P(('groups', 'wide')), parts along dimension 0, may hold values from -0.75 to 0.75
- row_adapter_index: int32 [4096, 1], P(('groups', 'wide')), parts along dimension 0, may hold values from 0 to 15; in each aligned block of 128 rows (0 to 127, 128 to 255, ...) at most 16 rows name the same one
- device_adapter: int32 [32], P('groups'), parts along dimension 0, may hold values from 0 to 15, each once
Outputs:
- input_grad: bfloat16 [4096, 8192], P(('groups', 'wide')), parts along dimension 0
- grad_down: float32 [32, 8192, 64], P(('groups', 'wide')), parts along dimension 0
- grad_up: float32 [32, 64, 1024], P(('groups', 'wide')), parts along dimension 0
The draws below stay inside these ranges and needn't reach their ends.
There are 2 independent parts, one for each index of `groups`. The reference program is written for one: setup_inputs(seed, part) draws one part's arguments, and reference() takes and returns one part's arrays. A program takes and returns all parts, laid end to end along the dimension named above; an argument that names none is the same for every part. Nothing has to cross between parts.
Inputs may be any that keep to these rules, and one draw needn't show every extreme that they name: `row_adapter_index`: no adapter is named by more than 16 rows of one device, and on every draw some adapter is named by exactly 16 rows of some device. `device_adapter`: each adapter is held by exactly one device.
All inputs are finite; a program needn't handle non-finite values.
Results may differ from the reference program's by a relative error of at most 0.0056.
Values may be sent and summed in bfloat16 or wider, within the bound.
No kernel may reach another device: no remote copies, remote signals or barrier semaphores. Data moves between devices by JAX's collectives and lax.ppermute only.
A program may use at most 128 MiB of HBM per device.

```python
import math
import jax
import jax.numpy as jnp
import numpy as np
from jax import lax

MODEL_WIDTH = 8192
KEY_FEATURES = 1024
ADAPTER_RANK = 64
TOK_DEV = 128
CAP = 16
TENANT_ADAPTERS = 16
TOKENS = 2048
N_WIDE = 16


def block_levels(rng, extent, shards, smallest, high):
    level, own = 1.0, jax.random.fold_in(rng, 6)
    for dim, shards_of in shards:
        draws = jnp.exp(jax.random.uniform(jax.random.fold_in(own, dim), (shards_of,), jnp.float32, smallest / len(shards), high / len(shards)))
        level = level * jnp.repeat(draws, extent[dim] // shards_of).reshape([-1 if axis == dim else 1 for axis in range(len(extent))])
    return level


def routed_block(own_key, own, number, rows, amount, top, bound, lean):
    ranking = jax.random.permutation(own_key, amount)
    heavy_load, ordinary = portions_of(amount, rows * top, bound, lean, True), portions_of(amount, rows * top, bound, lean, False)
    places = jnp.arange(amount)

    def named(sizes, rotation):
        used = int((sizes > 0).sum())
        fixed = max(1, used // 4)
        moved = fixed + (places - fixed + rotation * (used - fixed)) % max(1, amount - fixed)
        return jnp.zeros((amount,), jnp.int32).at[ranking[jnp.where(places < fixed, places, moved)]].set(jnp.asarray(sizes, jnp.int32))

    sizes = jnp.where(number % 4 == 0, named(heavy_load, number // 4), named(ordinary, number - number // 4 - 1))
    mixed = jax.random.permutation(jax.random.fold_in(own, 3), amount)
    giver, taker = mixed[0:amount // 2 * 2:2], mixed[1:amount // 2 * 2:2]
    slack = jnp.minimum(sizes[giver] - 1, bound - sizes[taker]) // 2
    slack = jnp.where((giver == ranking[0]) | (taker == ranking[0]) | (sizes[taker] == 0), 0, jnp.maximum(slack, 0))
    moved = jax.random.randint(jax.random.fold_in(own, 4), (amount // 2,), 0, 1 << 20) % (slack + 1)
    sizes = sizes.at[giver].add(-moved).at[taker].add(moved)
    members = jnp.searchsorted(jnp.cumsum(sizes), jnp.arange(rows * top), side="right").astype(jnp.int32)
    listing = members.reshape(top, rows).T
    listing = listing[jax.random.permutation(jax.random.fold_in(own, 1), rows)]
    rotation = jax.random.randint(jax.random.fold_in(own, 2), (rows, 1), 0, top)
    return jnp.take_along_axis(listing, (jnp.arange(top)[None, :] + rotation) % top, axis=1)


def portions_of(amount, total, bound, skew, full):
    loads = [(1 << 20) // math.isqrt(grade ** skew) + 1 for grade in range(1, amount + 1)]
    largest = bound if full else min(bound, max(-(-total // amount), total * loads[0] // sum(loads)))
    least = 1 if total - largest >= amount - 1 else 0
    given, surplus = [largest] + [least] * (amount - 1), total - largest - least * (amount - 1)
    while surplus > 0:
        movable = [i for i in range(1, amount) if given[i] < largest] or [i for i in range(1, amount) if given[i] < bound]
        whole, budget = sum([loads[i] for i in movable]), surplus
        for i in movable:
            addition = min(bound - given[i], max(1, budget * loads[i] // whole), surplus)
            given[i] = given[i] + addition
            surplus = surplus - addition
    return np.array(given)


def noise(own_key, dims, width, most, shards=(), kind=jnp.bfloat16):
    level = block_levels(own_key, dims, shards, -0.22, 0.18) if shards else 1.0
    entries = jax.random.normal(own_key, dims, jnp.float32) * width * level
    return jnp.minimum(jnp.maximum(entries, -most), most).astype(kind)


def setup_inputs(seed: int = 0, part: int = 0) -> dict:
    streams_of = jax.random.split(jax.random.key(seed), 8)
    part_keys = jax.random.split(jax.random.fold_in(streams_of[7], part), 8)
    features = noise(part_keys[0], (TOKENS, MODEL_WIDTH), 1.0, 6.0, ((0, 16),))
    cotangent = noise(part_keys[1], (TOKENS, KEY_FEATURES), 1.0, 6.0, ((0, 16),))
    frozen_key_weight = noise(streams_of[2], (MODEL_WIDTH, KEY_FEATURES), MODEL_WIDTH ** -0.5, 0.0625, ((0, 16),))
    adapter_down_weight = noise(part_keys[3], (TENANT_ADAPTERS, MODEL_WIDTH, ADAPTER_RANK), MODEL_WIDTH ** -0.5, 0.0625, ((0, 16),))
    adapter_up_weight = noise(part_keys[4], (TENANT_ADAPTERS, ADAPTER_RANK, KEY_FEATURES), ADAPTER_RANK ** -0.5, 0.75, ((0, 16),))
    row_adapter_index_keys = jax.random.split(jax.random.fold_in(part_keys[5], 1), TOKENS // TOK_DEV)
    row_adapter_index_turns = jax.random.permutation(jax.random.fold_in(part_keys[5], 3), TOKENS // TOK_DEV)
    row_adapter_index = jax.vmap(lambda own, number: routed_block(jax.random.fold_in(part_keys[5], 2), own, number, TOK_DEV, TENANT_ADAPTERS, 1, CAP, 2))(row_adapter_index_keys, row_adapter_index_turns).reshape((TOKENS, 1))
    device_adapter = jax.random.permutation(part_keys[6], TENANT_ADAPTERS).astype(jnp.int32)
    return {"features": features, "cotangent": cotangent, "frozen_key_weight": frozen_key_weight, "adapter_down_weight": adapter_down_weight, "adapter_up_weight": adapter_up_weight, "row_adapter_index": row_adapter_index, "device_adapter": device_adapter}


adapter_scale = 2.0


def reference(features, cotangent, frozen_key_weight, adapter_down_weight, adapter_up_weight, row_adapter_index, device_adapter):
    slot_index = jnp.arange(TENANT_ADAPTERS, dtype=jnp.int32)
    slot_of = jnp.zeros((TENANT_ADAPTERS,), jnp.int32).at[device_adapter].set(slot_index)
    token_slot = slot_of[row_adapter_index[:, 0]].astype(jnp.int32)
    base_grad = jnp.dot(cotangent, frozen_key_weight.T, preferred_element_type=jnp.float32)
    order = jnp.argsort(token_slot, stable=True).astype(jnp.int32)
    token_counts = jnp.zeros((TENANT_ADAPTERS,), jnp.int32).at[token_slot].add(1)
    starts = (jnp.cumsum(token_counts) - token_counts).astype(jnp.int32)
    most = N_WIDE * CAP
    offsets = jnp.arange(most, dtype=jnp.int32)

    def one_slot(carry, slot_position):
        index = jnp.minimum(starts[slot_position] + offsets, TOKENS - 1).astype(jnp.int32)
        live = offsets < token_counts[slot_position]
        rows = order[index]
        picked_in = jnp.where(live[:, None], features[rows], jnp.zeros((), jnp.bfloat16))
        picked_cot = jnp.where(live[:, None], cotangent[rows], jnp.zeros((), jnp.bfloat16))
        down_projection = adapter_down_weight[slot_position]
        up_projection = adapter_up_weight[slot_position]
        low_in = jnp.dot(picked_in, down_projection, preferred_element_type=jnp.float32).astype(jnp.bfloat16)
        low_rank_output = jnp.dot(picked_cot, up_projection.T, preferred_element_type=jnp.float32).astype(jnp.bfloat16)
        rows_per_adapter = (adapter_scale * jnp.dot(low_rank_output, down_projection.T, preferred_element_type=jnp.float32)).astype(jnp.bfloat16)
        rows_per_adapter = jnp.where(live[:, None], rows_per_adapter, jnp.zeros((), jnp.bfloat16))
        inverse_permutation = adapter_scale / jnp.maximum(token_counts[slot_position], 1).astype(jnp.float32)
        grad_down = inverse_permutation * jnp.dot(picked_in.T, low_rank_output, preferred_element_type=jnp.float32)
        grad_up = inverse_permutation * jnp.dot(low_in.T, picked_cot, preferred_element_type=jnp.float32)
        carry = carry.at[rows].add(rows_per_adapter)
        return carry, (grad_down, grad_up)

    start = jnp.zeros((TOKENS, MODEL_WIDTH), jnp.bfloat16)
    adapter_grad, grads = lax.scan(one_slot, start, slot_index)
    input_grad = (base_grad + adapter_grad.astype(jnp.float32)).astype(jnp.bfloat16)
    return input_grad, grads[0], grads[1]
```

```python
import jax
import jax.numpy as jnp
from jax import lax
from jax.experimental import pallas as pl
from jax.experimental.pallas import tpu as pltpu
from jax.sharding import PartitionSpec as P

adapter_scale = 2.0
LANES = 128
INDEX_ROWS = 16
STEP = 4
VMEM_BYTES = 40 * 1024 * 1024


def contract_matrices(left, right, left_dim, right_dim):
    return lax.dot_general(
        left, right, (((left_dim,), (right_dim,)), ((), ())), preferred_element_type=jnp.float32
    )


def frozen_part(cotangent, frozen_key_weight):
    return contract_matrices(
        cotangent, lax.all_gather(frozen_key_weight, "wide", axis=0, tiled=True), 1, 1
    )


def dispatch_body(
    features,
    cotangent,
    frozen_key_weight,
    adapter_down_weight,
    adapter_up_weight,
    row_adapter_index,
    device_adapter,
):
    row_count = features.shape[0]
    peer_count = lax.axis_size("wide")
    device_index = lax.axis_index("wide")
    capacity = max(2, 2 * row_count // peer_count)
    slot_range = jnp.arange(peer_count, dtype=jnp.int32)
    matches = row_adapter_index[:, 0][:, None] == device_adapter[None, :]
    token_slot = jnp.sum(jnp.where(matches, slot_range[None, :], 0), axis=1)
    slot_hit = (token_slot[:, None] == slot_range[None, :]).astype(jnp.int32)
    local_counts = jnp.sum(slot_hit, axis=0)
    token_counts = lax.psum(local_counts, "wide")
    earlier = jnp.cumsum(slot_hit, axis=0) - slot_hit
    token_rank = jnp.sum(earlier * slot_hit, axis=1)
    position = token_slot * capacity + token_rank
    slot_total = peer_count * capacity
    pick = position[None, :] == jnp.arange(slot_total, dtype=jnp.int32)[:, None]
    source_row = jnp.sum(
        jnp.where(pick, jnp.arange(row_count, dtype=jnp.int32)[None, :], 0), axis=1
    )
    filled = jnp.any(pick, axis=1)
    zero_value = jnp.zeros((), jnp.bfloat16)
    send_in = jnp.where(filled[:, None], features[source_row], zero_value).reshape(
        peer_count, capacity, -1
    )
    send_cot = jnp.where(filled[:, None], cotangent[source_row], zero_value).reshape(
        peer_count, capacity, -1
    )
    recv_in, recv_cot = (
        lax.all_to_all(send_in, "wide", split_axis=0, concat_axis=0, tiled=True),
        lax.all_to_all(send_cot, "wide", split_axis=0, concat_axis=0, tiled=True),
    )
    recv_in = recv_in.reshape(slot_total, -1)
    recv_cot = recv_cot.reshape(slot_total, -1)
    down_projection = adapter_down_weight[0]
    up_projection = adapter_up_weight[0]
    low_in = jnp.dot(recv_in, down_projection, preferred_element_type=jnp.float32).astype(
        jnp.bfloat16
    )
    low_rank_output = contract_matrices(recv_cot, up_projection, 1, 1).astype(jnp.bfloat16)
    rows_per_adapter = (
        adapter_scale * contract_matrices(low_rank_output, down_projection, 1, 1)
    ).astype(jnp.bfloat16)
    inverse_permutation = adapter_scale / jnp.maximum(token_counts[device_index], 1).astype(
        jnp.float32
    )
    grad_down = inverse_permutation * contract_matrices(recv_in, low_rank_output, 0, 0)
    grad_up = inverse_permutation * contract_matrices(low_in, recv_cot, 0, 0)
    returned = lax.all_to_all(
        rows_per_adapter.reshape(peer_count, capacity, -1),
        "wide",
        split_axis=0,
        concat_axis=0,
        tiled=True,
    )
    returned = returned.reshape(slot_total, -1)
    adapter_grad = returned[position]
    base_grad = frozen_part(cotangent, frozen_key_weight)
    input_grad = (base_grad + adapter_grad.astype(jnp.float32)).astype(jnp.bfloat16)
    return (input_grad, grad_down[None], grad_up[None])


def params():
    return pltpu.CompilerParams(vmem_limit_bytes=VMEM_BYTES)


def index_columns(packed):
    values = packed.astype(jnp.float32)
    chunks = packed.shape[2] // LANES
    return jnp.concatenate(
        [
            values[item, :, j * LANES : (j + 1) * LANES]
            for item in range(packed.shape[0])
            for j in range(chunks)
        ],
        axis=0,
    )


def pack_kernel(features_ref, down_ref, out_ref):
    rows = features_ref.shape[0]
    out_ref[0, :rows, :] = features_ref[...]
    out_ref[0, rows:, :] = down_ref[...]


def pack_columns(features, down, peer_count):
    rows, width = features.shape
    rank = down.shape[0]
    share = width // peer_count
    return pl.pallas_call(
        pack_kernel,
        grid=(peer_count,),
        in_specs=[
            pl.BlockSpec((rows, share), lambda d: (0, d)),
            pl.BlockSpec((rank, share), lambda d: (0, d)),
        ],
        out_specs=pl.BlockSpec((1, rows + rank, share), lambda d: (d, 0, 0)),
        out_shape=jax.ShapeDtypeStruct((peer_count, rows + rank, share), jnp.bfloat16),
        compiler_params=params(),
        cost_estimate=pl.CostEstimate(flops=0, bytes_accessed=6 << 20, transcendentals=0),
    )(features, down)


def low_out_kernel(cot_ref, up_ref, index_ref, weight_ref, ids_ref, low_ref, base_ref):
    keys = cot_ref.shape[2]
    cot = cot_ref[...].reshape(-1, keys)
    up = up_ref[...].reshape(-1, keys)
    low = contract_matrices(cot, up, 1, 1)
    column = index_columns(index_ref[...])
    for j in range(low.shape[1] // LANES):
        span = slice(j * LANES, (j + 1) * LANES)
        low_ref[:, span] = jnp.where(column == ids_ref[:, span], low[:, span], 0.0).astype(
            jnp.bfloat16
        )
    base_ref[...] = contract_matrices(cot, weight_ref[...], 1, 1)


def low_out(gathered, weight, ids, rows, rank):
    peer_count, _, keys = gathered.shape
    share = weight.shape[0]
    block = STEP * rows
    slots = peer_count * rank
    return pl.pallas_call(
        low_out_kernel,
        grid=(peer_count // STEP,),
        in_specs=[
            pl.BlockSpec((STEP, rows, keys), lambda s: (s, 0, 0)),
            pl.BlockSpec((peer_count, rank, keys), lambda s: (0, rows // rank, 0)),
            pl.BlockSpec(
                (STEP, INDEX_ROWS, keys), lambda s: (s, (rows + rank) // INDEX_ROWS, 0)
            ),
            pl.BlockSpec((share, keys), lambda s: (0, 0)),
            pl.BlockSpec((1, slots), lambda s: (0, 0)),
        ],
        out_specs=[
            pl.BlockSpec((block, slots), lambda s: (s, 0)),
            pl.BlockSpec((block, share), lambda s: (s, 0)),
        ],
        out_shape=[
            jax.ShapeDtypeStruct((peer_count * rows, slots), jnp.bfloat16),
            jax.ShapeDtypeStruct((peer_count * rows, share), jnp.float32),
        ],
        compiler_params=params(),
        cost_estimate=pl.CostEstimate(flops=7 << 30, bytes_accessed=16 << 20, transcendentals=0),
    )(gathered, gathered, gathered, weight, ids)


def share_kernel(feat_ref, down_ref, index_ref, low_ref, base_ref, ids_ref, out_ref):
    items, rows, share = feat_ref.shape
    down = down_ref[...].reshape(-1, share)
    grad = base_ref[...] + adapter_scale * contract_matrices(low_ref[...], down, 1, 0)
    out_ref[:, :rows, :] = grad.astype(jnp.bfloat16).reshape(items, rows, share)
    partial = contract_matrices(feat_ref[...].reshape(-1, share), down, 1, 1)
    column = index_columns(index_ref[...])
    total = jnp.zeros_like(column)
    for j in range(partial.shape[1] // LANES):
        span = slice(j * LANES, (j + 1) * LANES)
        total = total + jnp.where(column == ids_ref[:, span], partial[:, span], 0.0)
    total = total + pltpu.roll(total, LANES // 2, 1)
    left = lax.broadcasted_iota(jnp.int32, (INDEX_ROWS, LANES), 1) < LANES // 2
    for item in range(items):
        for j in range(rows // (2 * INDEX_ROWS)):
            first = item * rows + 2 * INDEX_ROWS * j
            middle = first + INDEX_ROWS
            pair = jnp.where(
                left, total[first:middle, :], total[middle : middle + INDEX_ROWS, :]
            )
            out_ref[item, rows:, j * LANES : (j + 1) * LANES] = pair.astype(jnp.bfloat16)


def share_results(received, gathered, low, base, ids, rows, rank):
    peer_count, _, share = received.shape
    keys = gathered.shape[2]
    block = STEP * rows
    slots = peer_count * rank
    return pl.pallas_call(
        share_kernel,
        grid=(peer_count // STEP,),
        in_specs=[
            pl.BlockSpec((STEP, rows, share), lambda s: (s, 0, 0)),
            pl.BlockSpec((peer_count, rank, share), lambda s: (0, rows // rank, 0)),
            pl.BlockSpec(
                (STEP, INDEX_ROWS, keys), lambda s: (s, (rows + rank) // INDEX_ROWS, 0)
            ),
            pl.BlockSpec((block, slots), lambda s: (s, 0)),
            pl.BlockSpec((block, share), lambda s: (s, 0)),
            pl.BlockSpec((1, slots), lambda s: (0, 0)),
        ],
        out_specs=pl.BlockSpec((STEP, rows + INDEX_ROWS, share), lambda s: (s, 0, 0)),
        out_shape=jax.ShapeDtypeStruct((peer_count, rows + INDEX_ROWS, share), jnp.bfloat16),
        compiler_params=params(),
        cost_estimate=pl.CostEstimate(flops=4 << 30, bytes_accessed=16 << 20, transcendentals=0),
    )(received, received, gathered, low, base, ids)


def finish_kernel(down_ref, low_ref, cot_ref, index_ref, own_ref, scale_ref, gd_ref, gu_ref, acc):
    step = pl.program_id(0)
    items, rank, share = down_ref.shape
    keys = cot_ref.shape[2]
    scale = scale_ref[0, 0]
    for item in range(items):
        gd_ref[:, item * share : (item + 1) * share] = scale * down_ref[item].astype(jnp.float32)
    pieces = []
    for item in range(items):
        for j in range(share // LANES):
            pair = low_ref[item, :, j * LANES : (j + 1) * LANES].astype(jnp.float32)
            pieces += [pair, pltpu.roll(pair, LANES // 2, 1)]
    low = jnp.concatenate(pieces, axis=0)
    column = index_columns(index_ref[...])
    low = jnp.where(column == own_ref[...], low, 0.0).astype(jnp.bfloat16)
    term = contract_matrices(low, cot_ref[...].reshape(-1, keys), 0, 0)

    @pl.when(step == 0)
    def _():
        acc[...] = jnp.zeros_like(acc)

    acc[...] += term

    @pl.when(step == pl.num_programs(0) - 1)
    def _():
        gu_ref[...] = scale * acc[:rank, :]


def finish(received, gathered, own, scale, rows, rank):
    peer_count, _, share = received.shape
    keys = gathered.shape[2]
    return pl.pallas_call(
        finish_kernel,
        grid=(peer_count // STEP,),
        in_specs=[
            pl.BlockSpec((STEP, rank, share), lambda s: (s, 0, 0)),
            pl.BlockSpec((STEP, INDEX_ROWS, share), lambda s: (s, rank // INDEX_ROWS, 0)),
            pl.BlockSpec((STEP, rows, keys), lambda s: (s, 0, 0)),
            pl.BlockSpec(
                (STEP, INDEX_ROWS, keys), lambda s: (s, (rows + rank) // INDEX_ROWS, 0)
            ),
            pl.BlockSpec((1, LANES), lambda s: (0, 0)),
            pl.BlockSpec((1, LANES), lambda s: (0, 0)),
        ],
        out_specs=[
            pl.BlockSpec((rank, STEP * share), lambda s: (0, s)),
            pl.BlockSpec((rank, keys), lambda s: (0, 0)),
        ],
        out_shape=[
            jax.ShapeDtypeStruct((rank, peer_count * share), jnp.float32),
            jax.ShapeDtypeStruct((rank, keys), jnp.float32),
        ],
        scratch_shapes=[pltpu.VMEM((LANES, keys), jnp.float32)],
        compiler_params=params(),
        cost_estimate=pl.CostEstimate(flops=1 << 29, bytes_accessed=8 << 20, transcendentals=0),
    )(received, received, gathered, gathered, own, scale)


def exchange(block):
    return lax.all_to_all(block, "wide", split_axis=0, concat_axis=0, tiled=True)


def column_body(
    features,
    cotangent,
    frozen_key_weight,
    adapter_down_weight,
    adapter_up_weight,
    row_adapter_index,
    device_adapter,
):
    rows, width = features.shape
    keys = cotangent.shape[1]
    rank = adapter_up_weight.shape[1]
    peer_count = lax.axis_size("wide")
    share = width // peer_count
    down = adapter_down_weight[0].T
    marks = jnp.broadcast_to(row_adapter_index.astype(jnp.bfloat16), (rows, LANES))
    marks = marks.reshape(rows // INDEX_ROWS, INDEX_ROWS, LANES).transpose(1, 0, 2)
    marks = marks.reshape(INDEX_ROWS, keys)
    payload = jnp.concatenate([cotangent, adapter_up_weight[0], marks], axis=0)
    gathered = lax.all_gather(payload, "wide", axis=0)
    received = exchange(pack_columns(features, down, peer_count))
    ids = jnp.repeat(device_adapter, rank)[None, :].astype(jnp.float32)
    low, base = low_out(gathered, frozen_key_weight, ids, rows, rank)
    results = exchange(share_results(received, gathered, low, base, ids, rows, rank))
    down_blocks = contract_matrices(low, received[:, :rows].reshape(-1, share), 0, 0)
    down_blocks = down_blocks.astype(jnp.bfloat16).reshape(peer_count, rank, share)
    low_in = jnp.sum(results[:, rows:].astype(jnp.float32), axis=0).astype(jnp.bfloat16)
    low_in = jnp.broadcast_to(low_in[None], (peer_count, INDEX_ROWS, share))
    last = exchange(jnp.concatenate([down_blocks, low_in], axis=1))
    input_grad = results[:, :rows].transpose(1, 0, 2).reshape(rows, width)
    own = device_adapter[lax.axis_index("wide")].astype(jnp.float32)
    hits = gathered[:, rows + rank :, :].astype(jnp.float32) == own
    count = jnp.sum(hits.astype(jnp.float32)) / LANES
    scale = jnp.full((1, LANES), adapter_scale, jnp.float32) / jnp.maximum(count, 1.0)
    grad_down, grad_up = finish(
        last, gathered, jnp.full((1, LANES), own, jnp.float32), scale, rows, rank
    )
    return (input_grad, grad_down.T[None], grad_up[None])


def solution(mesh):
    in_specs = (
        P(("groups", "wide"), None),
        P(("groups", "wide"), None),
        P("wide", None),
        P(("groups", "wide"), None, None),
        P(("groups", "wide"), None, None),
        P(("groups", "wide"), None),
        P("groups"),
    )
    out_specs = (
        P(("groups", "wide"), None),
        P(("groups", "wide"), None, None),
        P(("groups", "wide"), None, None),
    )

    def body(*arrays):
        rows, width = arrays[0].shape
        keys = arrays[1].shape[1]
        rank = arrays[4].shape[1]
        peer_count = mesh.shape["wide"]
        by_columns = (
            peer_count % STEP == 0
            and peer_count * rank <= keys
            and rank * 2 == LANES
            and rows == LANES
            and rows // INDEX_ROWS * LANES == keys
            and rows * rank == INDEX_ROWS * (width // peer_count)
        )
        return (column_body if by_columns else dispatch_body)(*arrays)

    return jax.shard_map(body, mesh=mesh, in_specs=in_specs, out_specs=out_specs, check_vma=False)
```

```python
import jax
import jax.numpy as jnp
from jax import lax
from jax.experimental import pallas as pl
from jax.experimental.pallas import tpu as pltpu
from jax.sharding import PartitionSpec as P

adapter_scale = 2.0
LANES = 128
INDEX_ROWS = 16
CAPACITY = 16
STEP = 4


def contract_matrices(left, right, left_dim, right_dim):
    return lax.dot_general(
        left, right, (((left_dim,), (right_dim,)), ((), ())), preferred_element_type=jnp.float32
    )


def frozen_part(cotangent, frozen_key_weight):
    return contract_matrices(
        cotangent, lax.all_gather(frozen_key_weight, "wide", axis=0, tiled=True), 1, 1
    )


def dispatch_body(
    features,
    cotangent,
    frozen_key_weight,
    adapter_down_weight,
    adapter_up_weight,
    row_adapter_index,
    device_adapter,
):
    row_count = features.shape[0]
    peer_count = lax.axis_size("wide")
    device_index = lax.axis_index("wide")
    capacity = max(2, 2 * row_count // peer_count)
    slot_range = jnp.arange(peer_count, dtype=jnp.int32)
    matches = row_adapter_index[:, 0][:, None] == device_adapter[None, :]
    token_slot = jnp.sum(jnp.where(matches, slot_range[None, :], 0), axis=1)
    slot_hit = (token_slot[:, None] == slot_range[None, :]).astype(jnp.int32)
    local_counts = jnp.sum(slot_hit, axis=0)
    token_counts = lax.psum(local_counts, "wide")
    earlier = jnp.cumsum(slot_hit, axis=0) - slot_hit
    token_rank = jnp.sum(earlier * slot_hit, axis=1)
    position = token_slot * capacity + token_rank
    slot_total = peer_count * capacity
    pick = position[None, :] == jnp.arange(slot_total, dtype=jnp.int32)[:, None]
    source_row = jnp.sum(
        jnp.where(pick, jnp.arange(row_count, dtype=jnp.int32)[None, :], 0), axis=1
    )
    filled = jnp.any(pick, axis=1)
    zero_value = jnp.zeros((), jnp.bfloat16)
    send_in = jnp.where(filled[:, None], features[source_row], zero_value).reshape(
        peer_count, capacity, -1
    )
    send_cot = jnp.where(filled[:, None], cotangent[source_row], zero_value).reshape(
        peer_count, capacity, -1
    )
    recv_in, recv_cot = (
        lax.all_to_all(send_in, "wide", split_axis=0, concat_axis=0, tiled=True),
        lax.all_to_all(send_cot, "wide", split_axis=0, concat_axis=0, tiled=True),
    )
    recv_in = recv_in.reshape(slot_total, -1)
    recv_cot = recv_cot.reshape(slot_total, -1)
    down_projection = adapter_down_weight[0]
    up_projection = adapter_up_weight[0]
    low_in = jnp.dot(recv_in, down_projection, preferred_element_type=jnp.float32).astype(
        jnp.bfloat16
    )
    low_rank_output = contract_matrices(recv_cot, up_projection, 1, 1).astype(jnp.bfloat16)
    rows_per_adapter = (
        adapter_scale * contract_matrices(low_rank_output, down_projection, 1, 1)
    ).astype(jnp.bfloat16)
    inverse_permutation = adapter_scale / jnp.maximum(token_counts[device_index], 1).astype(
        jnp.float32
    )
    grad_down = inverse_permutation * contract_matrices(recv_in, low_rank_output, 0, 0)
    grad_up = inverse_permutation * contract_matrices(low_in, recv_cot, 0, 0)
    returned = lax.all_to_all(
        rows_per_adapter.reshape(peer_count, capacity, -1),
        "wide",
        split_axis=0,
        concat_axis=0,
        tiled=True,
    )
    returned = returned.reshape(slot_total, -1)
    adapter_grad = returned[position]
    base_grad = frozen_part(cotangent, frozen_key_weight)
    input_grad = (base_grad + adapter_grad.astype(jnp.float32)).astype(jnp.bfloat16)
    return (input_grad, grad_down[None], grad_up[None])


def params(mebibytes):
    return pltpu.CompilerParams(vmem_limit_bytes=mebibytes * 1024 * 1024)


def place_columns(packed):
    values = packed.astype(jnp.float32)
    chunks = packed.shape[2] // LANES
    return jnp.concatenate(
        [
            values[item, :, j * LANES : (j + 1) * LANES]
            for item in range(packed.shape[0])
            for j in range(chunks)
        ],
        axis=0,
    )


def payload_kernel(cot_ref, up_ref, index_ref, adapters_ref, out_ref):
    rows = cot_ref.shape[0]
    rank = up_ref.shape[0]
    peers = adapters_ref.shape[0]
    out_ref[:rows, :] = cot_ref[...]
    out_ref[rows : rows + rank, :] = up_ref[...]
    index = index_ref[...]
    slot = jnp.zeros(index.shape, jnp.int32)
    for w in range(peers):
        slot = jnp.where(index == adapters_ref[w], w, slot)
    slot_range = lax.broadcasted_iota(jnp.int32, (peers, rows), 0)
    hits = jnp.where(slot_range == slot, 1.0, 0.0)
    before = lax.broadcasted_iota(jnp.int32, (rows, rows), 0)
    after = lax.broadcasted_iota(jnp.int32, (rows, rows), 1)
    earlier = jnp.where(before < after, 1.0, 0.0).astype(jnp.bfloat16)
    ranks = contract_matrices(hits.astype(jnp.bfloat16), earlier, 1, 0)
    order = jnp.sum(hits * ranks, axis=0, keepdims=True)
    place = slot.astype(jnp.float32) * CAPACITY + order
    marks = jnp.broadcast_to(place, (rows, rows)).T.astype(jnp.bfloat16)
    for j in range(rows // INDEX_ROWS):
        out_ref[rows + rank :, j * LANES : (j + 1) * LANES] = marks[
            j * INDEX_ROWS : (j + 1) * INDEX_ROWS, :
        ]


def build_payload(cotangent, up, index, adapters):
    total = cotangent.shape[0] + up.shape[0] + INDEX_ROWS
    vmem = pl.BlockSpec(memory_space=pltpu.VMEM)
    return pl.pallas_call(
        payload_kernel,
        in_specs=[vmem, vmem, vmem, pl.BlockSpec(memory_space=pltpu.SMEM)],
        out_shape=jax.ShapeDtypeStruct((total, cotangent.shape[1]), jnp.bfloat16),
        compiler_params=params(58),
        cost_estimate=pl.CostEstimate(flops=0, bytes_accessed=1 << 20, transcendentals=0),
    )(cotangent, up, index, adapters)


def pack_kernel(features_ref, down_ref, out_ref):
    rows = features_ref.shape[0]
    share = out_ref.shape[2]
    for d in range(out_ref.shape[0]):
        span = slice(d * share, (d + 1) * share)
        out_ref[d, :rows, :] = features_ref[:, span]
        out_ref[d, rows:, :] = down_ref[:, span]


def pack_columns(features, down, peer_count):
    rows, width = features.shape
    rank = down.shape[0]
    share = width // peer_count
    return pl.pallas_call(
        pack_kernel,
        grid=(peer_count // 2,),
        in_specs=[
            pl.BlockSpec((rows, 2 * share), lambda d: (0, d)),
            pl.BlockSpec((rank, 2 * share), lambda d: (0, d)),
        ],
        out_specs=pl.BlockSpec((2, rows + rank, share), lambda d: (d, 0, 0)),
        out_shape=jax.ShapeDtypeStruct((peer_count, rows + rank, share), jnp.bfloat16),
        compiler_params=params(58),
        cost_estimate=pl.CostEstimate(flops=0, bytes_accessed=6 << 20, transcendentals=0),
    )(features, down)


def adapter_lanes(j):
    lane = lax.broadcasted_iota(jnp.int32, (1, LANES), 1)
    return (2 * j + lane // (LANES // 2)).astype(jnp.float32)


def low_out_kernel(cot_ref, up_ref, place_ref, weight_ref, low_ref, base_ref):
    keys = cot_ref.shape[2]
    cot = cot_ref[...].reshape(-1, keys)
    slot = jnp.floor(place_columns(place_ref[...]) / CAPACITY)
    low = contract_matrices(cot, up_ref[...].reshape(-1, keys), 1, 1)
    for j in range(low.shape[1] // LANES):
        span = slice(j * LANES, (j + 1) * LANES)
        low_ref[:, span] = jnp.where(slot == adapter_lanes(j), low[:, span], 0.0).astype(
            jnp.bfloat16
        )
    base_ref[...] = contract_matrices(cot, weight_ref[...], 1, 1)


def low_out(gathered, weight, rows, rank):
    peer_count, _, keys = gathered.shape
    share = weight.shape[0]
    block = STEP * rows
    slots = peer_count * rank
    once = pl.Buffered(1)
    return pl.pallas_call(
        low_out_kernel,
        grid=(peer_count // STEP,),
        in_specs=[
            pl.BlockSpec((STEP, rows, keys), lambda s: (s, 0, 0)),
            pl.BlockSpec(
                (peer_count, rank, keys), lambda s: (0, rows // rank, 0), pipeline_mode=once
            ),
            pl.BlockSpec(
                (STEP, INDEX_ROWS, keys), lambda s: (s, (rows + rank) // INDEX_ROWS, 0)
            ),
            pl.BlockSpec((share, keys), lambda s: (0, 0), pipeline_mode=once),
        ],
        out_specs=[
            pl.BlockSpec((block, slots), lambda s: (s, 0)),
            pl.BlockSpec((block, share), lambda s: (s, 0)),
        ],
        out_shape=[
            jax.ShapeDtypeStruct((peer_count * rows, slots), jnp.bfloat16),
            jax.ShapeDtypeStruct((peer_count * rows, share), jnp.float32),
        ],
        compiler_params=params(58),
        cost_estimate=pl.CostEstimate(flops=7 << 30, bytes_accessed=16 << 20, transcendentals=0),
    )(gathered, gathered, gathered, weight)


def share_kernel(feat_ref, down_ref, place_ref, low_ref, base_ref, out_ref, grad_ref):
    step = pl.program_id(0)
    items, rows, share = feat_ref.shape
    peers, rank, _ = down_ref.shape
    down = down_ref[...].reshape(-1, share)
    feat = feat_ref[...].reshape(-1, share)
    low = low_ref[...]
    grad = base_ref[...] + adapter_scale * contract_matrices(low, down, 1, 0)
    out_ref[pl.ds(step * items, items), :rows, :] = grad.astype(jnp.bfloat16).reshape(
        items, rows, share
    )

    @pl.when(step == 0)
    def _():
        grad_ref[...] = contract_matrices(low, feat, 0, 0)

    @pl.when(step > 0)
    def _():
        grad_ref[...] += contract_matrices(low, feat, 0, 0)

    partial = contract_matrices(feat, down, 1, 1)
    place = place_columns(place_ref[...])
    slot = jnp.floor(place / CAPACITY)
    total = jnp.zeros_like(place)
    for j in range(partial.shape[1] // LANES):
        span = slice(j * LANES, (j + 1) * LANES)
        total = total + jnp.where(slot == adapter_lanes(j), partial[:, span], 0.0)
    total = (total + pltpu.roll(total, LANES // 2, 1)).astype(jnp.bfloat16)
    places = lax.broadcasted_iota(jnp.int32, (peers * CAPACITY, LANES), 0).astype(jnp.float32)
    picked = []
    for item in range(items):
        span = slice(item * rows, (item + 1) * rows)
        row = place[span, :].T[:1, :]
        pick = jnp.where(places == row, 1.0, 0.0).astype(jnp.bfloat16)
        picked.append(contract_matrices(pick, total[span, :], 1, 0))
    left = lax.broadcasted_iota(jnp.int32, (CAPACITY, LANES), 1) < LANES // 2
    lanes = pl.ds(pl.multiple_of(step * LANES, LANES), LANES)
    for w in range(peers):
        span = slice(w * CAPACITY, (w + 1) * CAPACITY)
        for half in range(2):
            pair = jnp.where(left, picked[half][span, :], picked[half + 2][span, :])
            first = rows + rank + half * CAPACITY
            out_ref[w, first : first + CAPACITY, lanes] = pair.astype(jnp.bfloat16)

    @pl.when(step == pl.num_programs(0) - 1)
    def _():
        for w in range(peers):
            out_ref[w, rows : rows + rank, :] = grad_ref[w * rank : (w + 1) * rank, :].astype(
                jnp.bfloat16
            )


def share_results(received, gathered, low, base, rows, rank):
    peer_count, _, share = received.shape
    keys = gathered.shape[2]
    block = STEP * rows
    slots = peer_count * rank
    total = rows + rank + 2 * CAPACITY
    once = pl.Buffered(1)
    return pl.pallas_call(
        share_kernel,
        grid=(peer_count // STEP,),
        in_specs=[
            pl.BlockSpec((STEP, rows, share), lambda s: (s, 0, 0)),
            pl.BlockSpec(
                (peer_count, rank, share), lambda s: (0, rows // rank, 0), pipeline_mode=once
            ),
            pl.BlockSpec(
                (STEP, INDEX_ROWS, keys), lambda s: (s, (rows + rank) // INDEX_ROWS, 0)
            ),
            pl.BlockSpec((block, slots), lambda s: (s, 0)),
            pl.BlockSpec((block, share), lambda s: (s, 0)),
        ],
        out_specs=pl.BlockSpec((peer_count, total, share), lambda s: (0, 0, 0)),
        out_shape=jax.ShapeDtypeStruct((peer_count, total, share), jnp.bfloat16),
        scratch_shapes=[pltpu.VMEM((slots, share), jnp.float32)],
        compiler_params=params(58),
        cost_estimate=pl.CostEstimate(flops=7 << 30, bytes_accessed=16 << 20, transcendentals=0),
    )(received, received, gathered, low, base)


def select_kernel(own_ref, cot_ref, place_ref, rows_ref, scale_ref):
    step = pl.program_id(0)
    items, rows, _ = cot_ref.shape
    place = place_columns(place_ref[...])
    first = own_ref[0] * CAPACITY
    wanted = first + lax.broadcasted_iota(jnp.int32, (CAPACITY, LANES), 0)
    wanted = wanted.astype(jnp.float32)

    @pl.when(step == 0)
    def _():
        scale_ref[...] = jnp.zeros_like(scale_ref)

    for item in range(items):
        row = place[item * rows : (item + 1) * rows, :].T[:1, :]
        pick = jnp.where(wanted == row, 1.0, 0.0)
        scale_ref[...] += jnp.sum(pick, axis=0, keepdims=True)
        chosen = contract_matrices(pick.astype(jnp.bfloat16), cot_ref[item], 1, 0)
        rows_ref[item * CAPACITY : (item + 1) * CAPACITY, :] = chosen.astype(jnp.bfloat16)

    @pl.when(step == pl.num_programs(0) - 1)
    def _():
        count = jnp.sum(scale_ref[...], axis=1, keepdims=True)
        scale_ref[...] = adapter_scale / jnp.maximum(jnp.broadcast_to(count, (1, LANES)), 1.0)


def select_rows(own, gathered, rows, rank):
    peer_count, _, keys = gathered.shape
    return pl.pallas_call(
        select_kernel,
        grid=(peer_count // STEP,),
        in_specs=[
            pl.BlockSpec(memory_space=pltpu.SMEM),
            pl.BlockSpec((STEP, rows, keys), lambda s: (s, 0, 0)),
            pl.BlockSpec(
                (STEP, INDEX_ROWS, keys), lambda s: (s, (rows + rank) // INDEX_ROWS, 0)
            ),
        ],
        out_specs=[
            pl.BlockSpec((STEP * CAPACITY, keys), lambda s: (s, 0)),
            pl.BlockSpec((1, LANES), lambda s: (0, 0)),
        ],
        out_shape=[
            jax.ShapeDtypeStruct((peer_count * CAPACITY, keys), jnp.bfloat16),
            jax.ShapeDtypeStruct((1, LANES), jnp.float32),
        ],
        compiler_params=params(58),
        cost_estimate=pl.CostEstimate(flops=1 << 29, bytes_accessed=8 << 20, transcendentals=0),
    )(own, gathered, gathered)


def finish_kernel(part_ref, cot_ref, scale_ref, grad_ref, gd_ref, gu_ref, acc):
    step = pl.program_id(0)
    items, _, share = part_ref.shape
    rows = grad_ref.shape[0]
    rank = gd_ref.shape[0]
    scale = scale_ref[...]

    @pl.when(step == 0)
    def _():
        acc[...] = jnp.zeros_like(acc)

    for item in range(items):
        span = slice(item * share, (item + 1) * share)
        grad_ref[:, span] = part_ref[item, :rows, :]
        gd_ref[:, span] = scale[0, 0] * part_ref[item, rows : rows + rank, :].astype(jnp.float32)
        acc[...] += part_ref[item, rows + rank :, :].astype(jnp.float32)

    @pl.when(step == pl.num_programs(0) - 1)
    def _():
        pieces = []
        for source in range(cot_ref.shape[0] // CAPACITY):
            chunk, half, first = source // 4, source % 4 // 2, source % 2 * CAPACITY
            piece = acc[first : first + CAPACITY, chunk * LANES : (chunk + 1) * LANES]
            pieces.append(pltpu.roll(piece, LANES // 2, 1) if half else piece)
        low = jnp.concatenate(pieces, axis=0).astype(jnp.bfloat16)
        gu_ref[...] = scale[0, 0] * contract_matrices(low, cot_ref[...], 0, 0)[:rank, :]


def finish(parts, chosen, scale, rows, rank):
    peer_count, total, share = parts.shape
    slots, keys = chosen.shape
    return pl.pallas_call(
        finish_kernel,
        grid=(peer_count // STEP,),
        in_specs=[
            pl.BlockSpec((STEP, total, share), lambda s: (s, 0, 0)),
            pl.BlockSpec((slots, keys), lambda s: (0, 0)),
            pl.BlockSpec((1, LANES), lambda s: (0, 0)),
        ],
        out_specs=[
            pl.BlockSpec((rows, STEP * share), lambda s: (0, s)),
            pl.BlockSpec((rank, STEP * share), lambda s: (0, s)),
            pl.BlockSpec((rank, keys), lambda s: (0, 0)),
        ],
        out_shape=[
            jax.ShapeDtypeStruct((rows, peer_count * share), jnp.bfloat16),
            jax.ShapeDtypeStruct((rank, peer_count * share), jnp.float32),
            jax.ShapeDtypeStruct((rank, keys), jnp.float32),
        ],
        scratch_shapes=[pltpu.VMEM((2 * CAPACITY, share), jnp.float32)],
        compiler_params=params(58),
        cost_estimate=pl.CostEstimate(flops=1 << 27, bytes_accessed=8 << 20, transcendentals=0),
    )(parts, chosen, scale)


def swap(block, mask):
    peer_count = lax.axis_size("wide")
    return lax.ppermute(block, "wide", [(i, i ^ mask) for i in range(peer_count)])


def spread(payload, packed):
    far, near, beside, core = 12, 4, 2, 1
    mirrored, packed = lax.optimization_barrier((swap(payload, far), packed))
    held = [(0, payload), (far, mirrored)]
    for mask in (near, beside, core):
        held = held + [(shift ^ mask, swap(block, mask)) for shift, block in held]
    return lax.optimization_barrier((packed, held))


def exchange(block):
    return lax.all_to_all(block, "wide", split_axis=0, concat_axis=0, tiled=True)


def column_body(
    features,
    cotangent,
    frozen_key_weight,
    adapter_down_weight,
    adapter_up_weight,
    row_adapter_index,
    device_adapter,
):
    rows = features.shape[0]
    rank = adapter_up_weight.shape[1]
    peer_count = lax.axis_size("wide")
    device_index = lax.axis_index("wide")
    payload = build_payload(
        cotangent, adapter_up_weight[0], row_adapter_index.reshape(1, rows), device_adapter
    )
    packed = pack_columns(features, adapter_down_weight[0].T, peer_count)
    packed, held = spread(payload, packed)
    received = exchange(packed)
    gathered = jnp.zeros((peer_count,) + payload.shape, payload.dtype)
    for shift, block in held:
        gathered = lax.dynamic_update_slice(gathered, block[None], (device_index ^ shift, 0, 0))
    low, base = low_out(gathered, frozen_key_weight, rows, rank)
    parts = exchange(share_results(received, gathered, low, base, rows, rank))
    own = jnp.full((1,), device_index, jnp.int32)
    chosen, scale = select_rows(own, gathered, rows, rank)
    input_grad, grad_down, grad_up = finish(parts, chosen, scale, rows, rank)
    return (input_grad, grad_down.T[None], grad_up[None])


def solution(mesh):
    in_specs = (
        P(("groups", "wide"), None),
        P(("groups", "wide"), None),
        P("wide", None),
        P(("groups", "wide"), None, None),
        P(("groups", "wide"), None, None),
        P(("groups", "wide"), None),
        P("groups"),
    )
    out_specs = (
        P(("groups", "wide"), None),
        P(("groups", "wide"), None, None),
        P(("groups", "wide"), None, None),
    )

    def body(*arrays):
        rows, width = arrays[0].shape
        keys = arrays[1].shape[1]
        rank = arrays[4].shape[1]
        peer_count = mesh.shape["wide"]
        by_columns = (
            peer_count == STEP * STEP
            and peer_count * rank <= keys
            and rank * 2 == LANES
            and rows == LANES
            and rows // INDEX_ROWS * LANES == keys
            and peer_count * rank == 2 * (width // peer_count)
        )
        return (column_body if by_columns else dispatch_body)(*arrays)

    return jax.shard_map(body, mesh=mesh, in_specs=in_specs, out_specs=out_specs, check_vma=False)
```

```python
import jax
import jax.numpy as jnp
from jax import lax
from jax.experimental import pallas as pl
from jax.experimental.pallas import tpu as pltpu
from jax.sharding import PartitionSpec as P

adapter_scale = 2.0
LANES = 128
INDEX_ROWS = 16
CAPACITY = 16
STEP = 4


def contract_matrices(left, right, left_dim, right_dim):
    return lax.dot_general(
        left, right, (((left_dim,), (right_dim,)), ((), ())), preferred_element_type=jnp.float32
    )


def frozen_part(cotangent, frozen_key_weight):
    return contract_matrices(
        cotangent, lax.all_gather(frozen_key_weight, "wide", axis=0, tiled=True), 1, 1
    )


def dispatch_body(
    features,
    cotangent,
    frozen_key_weight,
    adapter_down_weight,
    adapter_up_weight,
    row_adapter_index,
    device_adapter,
):
    row_count = features.shape[0]
    peer_count = lax.axis_size("wide")
    device_index = lax.axis_index("wide")
    capacity = max(2, 2 * row_count // peer_count)
    slot_range = jnp.arange(peer_count, dtype=jnp.int32)
    matches = row_adapter_index[:, 0][:, None] == device_adapter[None, :]
    token_slot = jnp.sum(jnp.where(matches, slot_range[None, :], 0), axis=1)
    slot_hit = (token_slot[:, None] == slot_range[None, :]).astype(jnp.int32)
    local_counts = jnp.sum(slot_hit, axis=0)
    token_counts = lax.psum(local_counts, "wide")
    earlier = jnp.cumsum(slot_hit, axis=0) - slot_hit
    token_rank = jnp.sum(earlier * slot_hit, axis=1)
    position = token_slot * capacity + token_rank
    slot_total = peer_count * capacity
    pick = position[None, :] == jnp.arange(slot_total, dtype=jnp.int32)[:, None]
    source_row = jnp.sum(
        jnp.where(pick, jnp.arange(row_count, dtype=jnp.int32)[None, :], 0), axis=1
    )
    filled = jnp.any(pick, axis=1)
    zero_value = jnp.zeros((), jnp.bfloat16)
    send_in = jnp.where(filled[:, None], features[source_row], zero_value).reshape(
        peer_count, capacity, -1
    )
    send_cot = jnp.where(filled[:, None], cotangent[source_row], zero_value).reshape(
        peer_count, capacity, -1
    )
    recv_in, recv_cot = (
        lax.all_to_all(send_in, "wide", split_axis=0, concat_axis=0, tiled=True),
        lax.all_to_all(send_cot, "wide", split_axis=0, concat_axis=0, tiled=True),
    )
    recv_in = recv_in.reshape(slot_total, -1)
    recv_cot = recv_cot.reshape(slot_total, -1)
    down_projection = adapter_down_weight[0]
    up_projection = adapter_up_weight[0]
    low_in = jnp.dot(recv_in, down_projection, preferred_element_type=jnp.float32).astype(
        jnp.bfloat16
    )
    low_rank_output = contract_matrices(recv_cot, up_projection, 1, 1).astype(jnp.bfloat16)
    rows_per_adapter = (
        adapter_scale * contract_matrices(low_rank_output, down_projection, 1, 1)
    ).astype(jnp.bfloat16)
    inverse_permutation = adapter_scale / jnp.maximum(token_counts[device_index], 1).astype(
        jnp.float32
    )
    grad_down = inverse_permutation * contract_matrices(recv_in, low_rank_output, 0, 0)
    grad_up = inverse_permutation * contract_matrices(low_in, recv_cot, 0, 0)
    returned = lax.all_to_all(
        rows_per_adapter.reshape(peer_count, capacity, -1),
        "wide",
        split_axis=0,
        concat_axis=0,
        tiled=True,
    )
    returned = returned.reshape(slot_total, -1)
    adapter_grad = returned[position]
    base_grad = frozen_part(cotangent, frozen_key_weight)
    input_grad = (base_grad + adapter_grad.astype(jnp.float32)).astype(jnp.bfloat16)
    return (input_grad, grad_down[None], grad_up[None])


def params(mebibytes):
    return pltpu.CompilerParams(vmem_limit_bytes=mebibytes * 1024 * 1024)


def place_columns(packed):
    values = packed.astype(jnp.float32)
    chunks = packed.shape[2] // LANES
    return jnp.concatenate(
        [
            values[item, :, j * LANES : (j + 1) * LANES]
            for item in range(packed.shape[0])
            for j in range(chunks)
        ],
        axis=0,
    )


def payload_kernel(cot_ref, up_ref, index_ref, adapters_ref, out_ref):
    rows = cot_ref.shape[0]
    rank = up_ref.shape[0]
    peers = adapters_ref.shape[0]
    out_ref[:rows, :] = cot_ref[...]
    out_ref[rows : rows + rank, :] = up_ref[...]
    index = index_ref[...]
    slot = jnp.zeros(index.shape, jnp.int32)
    for w in range(peers):
        slot = jnp.where(index == adapters_ref[w], w, slot)
    slot_range = lax.broadcasted_iota(jnp.int32, (peers, rows), 0)
    hits = jnp.where(slot_range == slot, 1.0, 0.0)
    before = lax.broadcasted_iota(jnp.int32, (rows, rows), 0)
    after = lax.broadcasted_iota(jnp.int32, (rows, rows), 1)
    earlier = jnp.where(before < after, 1.0, 0.0).astype(jnp.bfloat16)
    ranks = contract_matrices(hits.astype(jnp.bfloat16), earlier, 1, 0)
    order = jnp.sum(hits * ranks, axis=0, keepdims=True)
    place = slot.astype(jnp.float32) * CAPACITY + order
    marks = jnp.broadcast_to(place, (rows, rows)).T.astype(jnp.bfloat16)
    for j in range(rows // INDEX_ROWS):
        out_ref[rows + rank :, j * LANES : (j + 1) * LANES] = marks[
            j * INDEX_ROWS : (j + 1) * INDEX_ROWS, :
        ]


def build_payload(cotangent, up, index, adapters):
    total = cotangent.shape[0] + up.shape[0] + INDEX_ROWS
    vmem = pl.BlockSpec(memory_space=pltpu.VMEM)
    return pl.pallas_call(
        payload_kernel,
        in_specs=[vmem, vmem, vmem, pl.BlockSpec(memory_space=pltpu.SMEM)],
        out_shape=jax.ShapeDtypeStruct((total, cotangent.shape[1]), jnp.bfloat16),
        compiler_params=params(56),
        cost_estimate=pl.CostEstimate(flops=0, bytes_accessed=1 << 20, transcendentals=0),
    )(cotangent, up, index, adapters)


def pack_kernel(features_ref, down_ref, out_ref):
    rows = features_ref.shape[0]
    share = out_ref.shape[2]
    for d in range(out_ref.shape[0]):
        span = slice(d * share, (d + 1) * share)
        out_ref[d, :rows, :] = features_ref[:, span]
        out_ref[d, rows:, :] = down_ref[:, span]


def pack_columns(features, down, peer_count):
    rows, width = features.shape
    rank = down.shape[0]
    share = width // peer_count
    return pl.pallas_call(
        pack_kernel,
        grid=(peer_count // 2,),
        in_specs=[
            pl.BlockSpec((rows, 2 * share), lambda d: (0, d)),
            pl.BlockSpec((rank, 2 * share), lambda d: (0, d)),
        ],
        out_specs=pl.BlockSpec((2, rows + rank, share), lambda d: (d, 0, 0)),
        out_shape=jax.ShapeDtypeStruct((peer_count, rows + rank, share), jnp.bfloat16),
        compiler_params=params(56),
        cost_estimate=pl.CostEstimate(flops=0, bytes_accessed=6 << 20, transcendentals=0),
    )(features, down)


def adapter_lanes(j):
    lane = lax.broadcasted_iota(jnp.int32, (1, LANES), 1)
    return (2 * j + lane // (LANES // 2)).astype(jnp.float32)


def low_out_kernel(cot_ref, up_ref, place_ref, weight_ref, low_ref, base_ref):
    keys = cot_ref.shape[2]
    cot = cot_ref[...].reshape(-1, keys)
    slot = jnp.floor(place_columns(place_ref[...]) / CAPACITY)
    low = contract_matrices(cot, up_ref[...].reshape(-1, keys), 1, 1)
    total = jnp.zeros_like(slot)
    for j in range(low.shape[1] // LANES):
        span = slice(j * LANES, (j + 1) * LANES)
        total = total + jnp.where(slot == adapter_lanes(j), low[:, span], 0.0)
    low_ref[...] = (total + pltpu.roll(total, LANES // 2, 1)).astype(jnp.bfloat16)
    base_ref[...] = contract_matrices(cot, weight_ref[...], 1, 1)


def low_out(gathered, weight, rows, rank):
    peer_count, _, keys = gathered.shape
    share = weight.shape[0]
    block = STEP * rows
    once = pl.Buffered(1)
    return pl.pallas_call(
        low_out_kernel,
        grid=(peer_count // STEP,),
        in_specs=[
            pl.BlockSpec((STEP, rows, keys), lambda s: (s, 0, 0)),
            pl.BlockSpec(
                (peer_count, rank, keys), lambda s: (0, rows // rank, 0), pipeline_mode=once
            ),
            pl.BlockSpec(
                (STEP, INDEX_ROWS, keys), lambda s: (s, (rows + rank) // INDEX_ROWS, 0)
            ),
            pl.BlockSpec((share, keys), lambda s: (0, 0), pipeline_mode=once),
        ],
        out_specs=[
            pl.BlockSpec((block, LANES), lambda s: (s, 0)),
            pl.BlockSpec((block, share), lambda s: (s, 0)),
        ],
        out_shape=[
            jax.ShapeDtypeStruct((peer_count * rows, LANES), jnp.bfloat16),
            jax.ShapeDtypeStruct((peer_count * rows, share), jnp.float32),
        ],
        compiler_params=params(56),
        cost_estimate=pl.CostEstimate(flops=7 << 30, bytes_accessed=16 << 20, transcendentals=0),
    )(gathered, gathered, gathered, weight)


def share_kernel(feat_ref, down_ref, place_ref, low_ref, base_ref, out_ref, grad_ref):
    step = pl.program_id(0)
    items, rows, share = feat_ref.shape
    peers, rank, _ = down_ref.shape

    @pl.when(step == 0)
    def _():
        grad_ref[...] = jnp.zeros_like(grad_ref)

    down = down_ref[...].reshape(-1, share)
    feat = feat_ref[...].reshape(-1, share)
    place = place_columns(place_ref[...])
    slot = jnp.floor(place / CAPACITY)
    folded = low_ref[...].astype(jnp.float32)
    partial = contract_matrices(feat, down, 1, 1)
    total = jnp.zeros_like(place)
    spread_low = []
    for j in range(partial.shape[1] // LANES):
        span = slice(j * LANES, (j + 1) * LANES)
        mine = slot == adapter_lanes(j)
        total = total + jnp.where(mine, partial[:, span], 0.0)
        spread_low.append(jnp.where(mine, folded, 0.0).astype(jnp.bfloat16))
    low = jnp.concatenate(spread_low, axis=1)
    grad_ref[...] += contract_matrices(low, feat, 0, 0)
    grad = base_ref[...] + adapter_scale * contract_matrices(low, down, 1, 0)
    out_ref[pl.ds(step * items, items), :rows, :] = grad.astype(jnp.bfloat16).reshape(
        items, rows, share
    )
    total = (total + pltpu.roll(total, LANES // 2, 1)).astype(jnp.bfloat16)
    places = lax.broadcasted_iota(jnp.int32, (peers * CAPACITY, LANES), 0).astype(jnp.float32)
    picked = []
    for item in range(items):
        span = slice(item * rows, (item + 1) * rows)
        row = place[span, :].T[:1, :]
        pick = jnp.where(places == row, 1.0, 0.0).astype(jnp.bfloat16)
        picked.append(contract_matrices(pick, total[span, :], 1, 0))
    left = lax.broadcasted_iota(jnp.int32, (CAPACITY, LANES), 1) < LANES // 2
    lanes = pl.ds(pl.multiple_of(step * LANES, LANES), LANES)
    for w in range(peers):
        span = slice(w * CAPACITY, (w + 1) * CAPACITY)
        for half in range(2):
            pair = jnp.where(left, picked[half][span, :], picked[half + 2][span, :])
            first = rows + rank + half * CAPACITY
            out_ref[w, first : first + CAPACITY, lanes] = pair.astype(jnp.bfloat16)

    @pl.when(step == pl.num_programs(0) - 1)
    def _():
        for w in range(peers):
            out_ref[w, rows : rows + rank, :] = grad_ref[w * rank : (w + 1) * rank, :].astype(
                jnp.bfloat16
            )


def share_results(received, gathered, low, base, rows, rank):
    peer_count, _, share = received.shape
    keys = gathered.shape[2]
    block = STEP * rows
    slots = peer_count * rank
    total = rows + rank + 2 * CAPACITY
    once = pl.Buffered(1)
    return pl.pallas_call(
        share_kernel,
        grid=(peer_count // STEP,),
        in_specs=[
            pl.BlockSpec((STEP, rows, share), lambda s: (s, 0, 0)),
            pl.BlockSpec(
                (peer_count, rank, share), lambda s: (0, rows // rank, 0), pipeline_mode=once
            ),
            pl.BlockSpec(
                (STEP, INDEX_ROWS, keys), lambda s: (s, (rows + rank) // INDEX_ROWS, 0)
            ),
            pl.BlockSpec((block, LANES), lambda s: (s, 0)),
            pl.BlockSpec((block, share), lambda s: (s, 0)),
        ],
        out_specs=pl.BlockSpec((peer_count, total, share), lambda s: (0, 0, 0)),
        out_shape=jax.ShapeDtypeStruct((peer_count, total, share), jnp.bfloat16),
        scratch_shapes=[pltpu.VMEM((slots, share), jnp.float32)],
        compiler_params=params(56),
        cost_estimate=pl.CostEstimate(flops=7 << 30, bytes_accessed=16 << 20, transcendentals=0),
    )(received, received, gathered, low, base)


def select_kernel(own_ref, cot_ref, place_ref, rows_ref, scale_ref):
    step = pl.program_id(0)
    items, rows, _ = cot_ref.shape
    place = place_columns(place_ref[...])
    first = own_ref[0] * CAPACITY
    wanted = first + lax.broadcasted_iota(jnp.int32, (CAPACITY, LANES), 0)
    wanted = wanted.astype(jnp.float32)

    @pl.when(step == 0)
    def _():
        scale_ref[...] = jnp.zeros_like(scale_ref)

    for item in range(items):
        row = place[item * rows : (item + 1) * rows, :].T[:1, :]
        pick = jnp.where(wanted == row, 1.0, 0.0)
        scale_ref[...] += jnp.sum(pick, axis=0, keepdims=True)
        chosen = contract_matrices(pick.astype(jnp.bfloat16), cot_ref[item], 1, 0)
        rows_ref[item * CAPACITY : (item + 1) * CAPACITY, :] = chosen.astype(jnp.bfloat16)

    @pl.when(step == pl.num_programs(0) - 1)
    def _():
        count = jnp.sum(scale_ref[...], axis=1, keepdims=True)
        scale_ref[...] = adapter_scale / jnp.maximum(jnp.broadcast_to(count, (1, LANES)), 1.0)


def select_rows(own, gathered, rows, rank):
    peer_count, _, keys = gathered.shape
    return pl.pallas_call(
        select_kernel,
        grid=(peer_count // STEP,),
        in_specs=[
            pl.BlockSpec(memory_space=pltpu.SMEM),
            pl.BlockSpec((STEP, rows, keys), lambda s: (s, 0, 0)),
            pl.BlockSpec(
                (STEP, INDEX_ROWS, keys), lambda s: (s, (rows + rank) // INDEX_ROWS, 0)
            ),
        ],
        out_specs=[
            pl.BlockSpec((STEP * CAPACITY, keys), lambda s: (s, 0)),
            pl.BlockSpec((1, LANES), lambda s: (0, 0)),
        ],
        out_shape=[
            jax.ShapeDtypeStruct((peer_count * CAPACITY, keys), jnp.bfloat16),
            jax.ShapeDtypeStruct((1, LANES), jnp.float32),
        ],
        compiler_params=params(56),
        cost_estimate=pl.CostEstimate(flops=1 << 29, bytes_accessed=8 << 20, transcendentals=0),
    )(own, gathered, gathered)


def finish_kernel(part_ref, cot_ref, scale_ref, grad_ref, gd_ref, gu_ref, acc):
    step = pl.program_id(0)
    items, _, share = part_ref.shape
    rows = grad_ref.shape[0]
    rank = gd_ref.shape[0]
    scale = scale_ref[...]

    @pl.when(step == 0)
    def _():
        acc[...] = jnp.zeros_like(acc)

    for item in range(items):
        span = slice(item * share, (item + 1) * share)
        grad_ref[:, span] = part_ref[item, :rows, :]
        gd_ref[:, span] = scale[0, 0] * part_ref[item, rows : rows + rank, :].astype(jnp.float32)
        acc[...] += part_ref[item, rows + rank :, :].astype(jnp.float32)

    @pl.when(step == pl.num_programs(0) - 1)
    def _():
        pieces = []
        for source in range(cot_ref.shape[0] // CAPACITY):
            chunk, half, first = source // 4, source % 4 // 2, source % 2 * CAPACITY
            piece = acc[first : first + CAPACITY, chunk * LANES : (chunk + 1) * LANES]
            pieces.append(pltpu.roll(piece, LANES // 2, 1) if half else piece)
        low = jnp.concatenate(pieces, axis=0).astype(jnp.bfloat16)
        gu_ref[...] = scale[0, 0] * contract_matrices(low, cot_ref[...], 0, 0)[:rank, :]


def finish(parts, chosen, scale, rows, rank):
    peer_count, total, share = parts.shape
    slots, keys = chosen.shape
    return pl.pallas_call(
        finish_kernel,
        grid=(peer_count // STEP,),
        in_specs=[
            pl.BlockSpec((STEP, total, share), lambda s: (s, 0, 0)),
            pl.BlockSpec((slots, keys), lambda s: (0, 0)),
            pl.BlockSpec((1, LANES), lambda s: (0, 0)),
        ],
        out_specs=[
            pl.BlockSpec((rows, STEP * share), lambda s: (0, s)),
            pl.BlockSpec((rank, STEP * share), lambda s: (0, s)),
            pl.BlockSpec((rank, keys), lambda s: (0, 0)),
        ],
        out_shape=[
            jax.ShapeDtypeStruct((rows, peer_count * share), jnp.bfloat16),
            jax.ShapeDtypeStruct((rank, peer_count * share), jnp.float32),
            jax.ShapeDtypeStruct((rank, keys), jnp.float32),
        ],
        scratch_shapes=[pltpu.VMEM((2 * CAPACITY, share), jnp.float32)],
        compiler_params=params(56),
        cost_estimate=pl.CostEstimate(flops=1 << 27, bytes_accessed=8 << 20, transcendentals=0),
    )(parts, chosen, scale)


def swap(block, mask):
    peer_count = lax.axis_size("wide")
    return lax.ppermute(block, "wide", [(i, i ^ mask) for i in range(peer_count)])


def spread(payload, packed):
    far, near, beside, core = 12, 4, 2, 1
    mirrored, packed = lax.optimization_barrier((swap(payload, far), packed))
    held = [(0, payload), (far, mirrored)]
    for mask in (near, beside, core):
        held = held + [(shift ^ mask, swap(block, mask)) for shift, block in held]
    for place in [6, 7]:
        shift, block = held[place]
        packed, block = lax.optimization_barrier((packed, block))
        held[place] = (shift, block)
    return packed, held


def exchange(block):
    return lax.all_to_all(block, "wide", split_axis=0, concat_axis=0, tiled=True)


def column_body(
    features,
    cotangent,
    frozen_key_weight,
    adapter_down_weight,
    adapter_up_weight,
    row_adapter_index,
    device_adapter,
):
    rows = features.shape[0]
    rank = adapter_up_weight.shape[1]
    peer_count = lax.axis_size("wide")
    device_index = lax.axis_index("wide")
    payload = build_payload(
        cotangent, adapter_up_weight[0], row_adapter_index.reshape(1, rows), device_adapter
    )
    packed = pack_columns(features, adapter_down_weight[0].T, peer_count)
    packed, held = spread(payload, packed)
    received = exchange(packed)
    gathered = jnp.zeros((peer_count,) + payload.shape, payload.dtype)
    for shift, block in held:
        gathered = lax.dynamic_update_slice(gathered, block[None], (device_index ^ shift, 0, 0))
    low, base = low_out(gathered, frozen_key_weight, rows, rank)
    parts = exchange(share_results(received, gathered, low, base, rows, rank))
    own = jnp.full((1,), device_index, jnp.int32)
    chosen, scale = select_rows(own, gathered, rows, rank)
    input_grad, grad_down, grad_up = finish(parts, chosen, scale, rows, rank)
    return (input_grad, grad_down.T[None], grad_up[None])


def solution(mesh):
    in_specs = (
        P(("groups", "wide"), None),
        P(("groups", "wide"), None),
        P("wide", None),
        P(("groups", "wide"), None, None),
        P(("groups", "wide"), None, None),
        P(("groups", "wide"), None),
        P("groups"),
    )
    out_specs = (
        P(("groups", "wide"), None),
        P(("groups", "wide"), None, None),
        P(("groups", "wide"), None, None),
    )

    def body(*arrays):
        rows, width = arrays[0].shape
        keys = arrays[1].shape[1]
        rank = arrays[4].shape[1]
        peer_count = mesh.shape["wide"]
        by_columns = (
            peer_count == STEP * STEP
            and peer_count * rank <= keys
            and rank * 2 == LANES
            and rows == LANES
            and rows // INDEX_ROWS * LANES == keys
            and peer_count * rank == 2 * (width // peer_count)
        )
        return (column_body if by_columns else dispatch_body)(*arrays)

    return jax.shard_map(body, mesh=mesh, in_specs=in_specs, out_specs=out_specs, check_vma=False)
```

```python
import jax
import jax.numpy as jnp
from jax import lax
from jax.experimental import pallas as pl
from jax.experimental.pallas import tpu as pltpu
from jax.sharding import PartitionSpec as P

adapter_scale = 2.0
LANES = 128
INDEX_ROWS = 16
CAPACITY = 16
STEP = 4
WIDE_STEP = 8


def contract_matrices(left, right, left_dim, right_dim):
    return lax.dot_general(
        left, right, (((left_dim,), (right_dim,)), ((), ())), preferred_element_type=jnp.float32
    )


def frozen_part(cotangent, frozen_key_weight):
    return contract_matrices(
        cotangent, lax.all_gather(frozen_key_weight, "wide", axis=0, tiled=True), 1, 1
    )


def dispatch_body(
    features,
    cotangent,
    frozen_key_weight,
    adapter_down_weight,
    adapter_up_weight,
    row_adapter_index,
    device_adapter,
):
    row_count = features.shape[0]
    peer_count = lax.axis_size("wide")
    device_index = lax.axis_index("wide")
    capacity = max(2, 2 * row_count // peer_count)
    slot_range = jnp.arange(peer_count, dtype=jnp.int32)
    matches = row_adapter_index[:, 0][:, None] == device_adapter[None, :]
    token_slot = jnp.sum(jnp.where(matches, slot_range[None, :], 0), axis=1)
    slot_hit = (token_slot[:, None] == slot_range[None, :]).astype(jnp.int32)
    local_counts = jnp.sum(slot_hit, axis=0)
    token_counts = lax.psum(local_counts, "wide")
    earlier = jnp.cumsum(slot_hit, axis=0) - slot_hit
    token_rank = jnp.sum(earlier * slot_hit, axis=1)
    position = token_slot * capacity + token_rank
    slot_total = peer_count * capacity
    pick = position[None, :] == jnp.arange(slot_total, dtype=jnp.int32)[:, None]
    source_row = jnp.sum(
        jnp.where(pick, jnp.arange(row_count, dtype=jnp.int32)[None, :], 0), axis=1
    )
    filled = jnp.any(pick, axis=1)
    zero_value = jnp.zeros((), jnp.bfloat16)
    send_in = jnp.where(filled[:, None], features[source_row], zero_value).reshape(
        peer_count, capacity, -1
    )
    send_cot = jnp.where(filled[:, None], cotangent[source_row], zero_value).reshape(
        peer_count, capacity, -1
    )
    recv_in, recv_cot = (
        lax.all_to_all(send_in, "wide", split_axis=0, concat_axis=0, tiled=True),
        lax.all_to_all(send_cot, "wide", split_axis=0, concat_axis=0, tiled=True),
    )
    recv_in = recv_in.reshape(slot_total, -1)
    recv_cot = recv_cot.reshape(slot_total, -1)
    down_projection = adapter_down_weight[0]
    up_projection = adapter_up_weight[0]
    low_in = jnp.dot(recv_in, down_projection, preferred_element_type=jnp.float32).astype(
        jnp.bfloat16
    )
    low_rank_output = contract_matrices(recv_cot, up_projection, 1, 1).astype(jnp.bfloat16)
    rows_per_adapter = (
        adapter_scale * contract_matrices(low_rank_output, down_projection, 1, 1)
    ).astype(jnp.bfloat16)
    inverse_permutation = adapter_scale / jnp.maximum(token_counts[device_index], 1).astype(
        jnp.float32
    )
    grad_down = inverse_permutation * contract_matrices(recv_in, low_rank_output, 0, 0)
    grad_up = inverse_permutation * contract_matrices(low_in, recv_cot, 0, 0)
    returned = lax.all_to_all(
        rows_per_adapter.reshape(peer_count, capacity, -1),
        "wide",
        split_axis=0,
        concat_axis=0,
        tiled=True,
    )
    returned = returned.reshape(slot_total, -1)
    adapter_grad = returned[position]
    base_grad = frozen_part(cotangent, frozen_key_weight)
    input_grad = (base_grad + adapter_grad.astype(jnp.float32)).astype(jnp.bfloat16)
    return (input_grad, grad_down[None], grad_up[None])


def params(mebibytes):
    return pltpu.CompilerParams(vmem_limit_bytes=mebibytes * 1024 * 1024)


def place_columns(packed):
    values = packed.astype(jnp.float32)
    chunks = packed.shape[2] // LANES
    return jnp.concatenate(
        [
            values[item, :, j * LANES : (j + 1) * LANES]
            for item in range(packed.shape[0])
            for j in range(chunks)
        ],
        axis=0,
    )


def payload_kernel(cot_ref, up_ref, index_ref, adapters_ref, out_ref):
    rows = cot_ref.shape[0]
    rank = up_ref.shape[0]
    peers = adapters_ref.shape[0]
    out_ref[:rows, :] = cot_ref[...]
    out_ref[rows : rows + rank, :] = up_ref[...]
    index = index_ref[...]
    slot = jnp.zeros(index.shape, jnp.int32)
    for w in range(peers):
        slot = jnp.where(index == adapters_ref[w], w, slot)
    slot_range = lax.broadcasted_iota(jnp.int32, (peers, rows), 0)
    hits = jnp.where(slot_range == slot, 1.0, 0.0)
    before = lax.broadcasted_iota(jnp.int32, (rows, rows), 0)
    after = lax.broadcasted_iota(jnp.int32, (rows, rows), 1)
    earlier = jnp.where(before < after, 1.0, 0.0).astype(jnp.bfloat16)
    ranks = contract_matrices(hits.astype(jnp.bfloat16), earlier, 1, 0)
    order = jnp.sum(hits * ranks, axis=0, keepdims=True)
    place = slot.astype(jnp.float32) * CAPACITY + order
    marks = jnp.broadcast_to(place, (rows, rows)).T.astype(jnp.bfloat16)
    for j in range(rows // INDEX_ROWS):
        out_ref[rows + rank :, j * LANES : (j + 1) * LANES] = marks[
            j * INDEX_ROWS : (j + 1) * INDEX_ROWS, :
        ]


def build_payload(cotangent, up, index, adapters):
    total = cotangent.shape[0] + up.shape[0] + INDEX_ROWS
    vmem = pl.BlockSpec(memory_space=pltpu.VMEM)
    return pl.pallas_call(
        payload_kernel,
        in_specs=[vmem, vmem, vmem, pl.BlockSpec(memory_space=pltpu.SMEM)],
        out_shape=jax.ShapeDtypeStruct((total, cotangent.shape[1]), jnp.bfloat16),
        compiler_params=params(56),
        cost_estimate=pl.CostEstimate(flops=0, bytes_accessed=1 << 20, transcendentals=0),
    )(cotangent, up, index, adapters)


def pack_kernel(features_ref, down_ref, out_ref):
    rows = features_ref.shape[0]
    share = out_ref.shape[2]
    for d in range(out_ref.shape[0]):
        span = slice(d * share, (d + 1) * share)
        out_ref[d, :rows, :] = features_ref[:, span]
        out_ref[d, rows:, :] = down_ref[:, span]


def pack_columns(features, down, peer_count):
    rows, width = features.shape
    rank = down.shape[0]
    share = width // peer_count
    return pl.pallas_call(
        pack_kernel,
        grid=(peer_count // 2,),
        in_specs=[
            pl.BlockSpec((rows, 2 * share), lambda d: (0, d)),
            pl.BlockSpec((rank, 2 * share), lambda d: (0, d)),
        ],
        out_specs=pl.BlockSpec((2, rows + rank, share), lambda d: (d, 0, 0)),
        out_shape=jax.ShapeDtypeStruct((peer_count, rows + rank, share), jnp.bfloat16),
        compiler_params=params(56),
        cost_estimate=pl.CostEstimate(flops=0, bytes_accessed=6 << 20, transcendentals=0),
    )(features, down)


def adapter_lanes(j):
    lane = lax.broadcasted_iota(jnp.int32, (1, LANES), 1)
    return (2 * j + lane // (LANES // 2)).astype(jnp.float32)


def low_out_kernel(cot_ref, up_ref, place_ref, weight_ref, low_ref, base_ref):
    keys = cot_ref.shape[2]
    cot = cot_ref[...].reshape(-1, keys)
    slot = jnp.floor(place_columns(place_ref[...]) / CAPACITY)
    low = contract_matrices(cot, up_ref[...].reshape(-1, keys), 1, 1)
    total = jnp.zeros_like(slot)
    for j in range(low.shape[1] // LANES):
        span = slice(j * LANES, (j + 1) * LANES)
        total = total + jnp.where(slot == adapter_lanes(j), low[:, span], 0.0)
    low_ref[...] = (total + pltpu.roll(total, LANES // 2, 1)).astype(jnp.bfloat16)
    base_ref[...] = contract_matrices(cot, weight_ref[...], 1, 1)


def low_out(gathered, weight, rows, rank):
    peer_count, _, keys = gathered.shape
    share = weight.shape[0]
    block = STEP * rows
    once = pl.Buffered(1)
    return pl.pallas_call(
        low_out_kernel,
        grid=(peer_count // STEP,),
        in_specs=[
            pl.BlockSpec((STEP, rows, keys), lambda s: (s, 0, 0)),
            pl.BlockSpec(
                (peer_count, rank, keys), lambda s: (0, rows // rank, 0), pipeline_mode=once
            ),
            pl.BlockSpec(
                (STEP, INDEX_ROWS, keys), lambda s: (s, (rows + rank) // INDEX_ROWS, 0)
            ),
            pl.BlockSpec((share, keys), lambda s: (0, 0), pipeline_mode=once),
        ],
        out_specs=[
            pl.BlockSpec((block, LANES), lambda s: (s, 0)),
            pl.BlockSpec((block, share), lambda s: (s, 0)),
        ],
        out_shape=[
            jax.ShapeDtypeStruct((peer_count * rows, LANES), jnp.bfloat16),
            jax.ShapeDtypeStruct((peer_count * rows, share), jnp.float32),
        ],
        compiler_params=params(56),
        cost_estimate=pl.CostEstimate(flops=7 << 30, bytes_accessed=16 << 20, transcendentals=0),
    )(gathered, gathered, gathered, weight)


def share_kernel(feat_ref, down_ref, place_ref, low_ref, base_ref, sent_ref, grad_ref, out_ref, sems):
    step = pl.program_id(0)
    items, rows, share = feat_ref.shape
    peers, rank, _ = down_ref.shape

    @pl.when(step == 0)
    def _():
        grad_ref[...] = jnp.zeros_like(grad_ref)

    down = down_ref[...].reshape(-1, share)
    feat = feat_ref[...].reshape(-1, share)
    place = place_columns(place_ref[...])
    slot = jnp.floor(place / CAPACITY)
    folded = low_ref[...].astype(jnp.float32)
    partial = contract_matrices(feat, down, 1, 1)
    total = jnp.zeros_like(place)
    spread_low = []
    for j in range(partial.shape[1] // LANES):
        span = slice(j * LANES, (j + 1) * LANES)
        mine = slot == adapter_lanes(j)
        total = total + jnp.where(mine, partial[:, span], 0.0)
        spread_low.append(jnp.where(mine, folded, 0.0).astype(jnp.bfloat16))
    low = jnp.concatenate(spread_low, axis=1)
    grad_ref[...] += contract_matrices(low, feat, 0, 0)
    grad = base_ref[...] + adapter_scale * contract_matrices(low, down, 1, 0)
    block = pl.ds(step * items, items)
    out_ref[block, :rows, :] = grad.astype(jnp.bfloat16).reshape(items, rows, share)
    pltpu.make_async_copy(
        out_ref.at[block, pl.ds(0, rows), :], sent_ref.at[block, pl.ds(0, rows), :], sems.at[step]
    ).start()
    total = (total + pltpu.roll(total, LANES // 2, 1)).astype(jnp.bfloat16)
    places = lax.broadcasted_iota(jnp.int32, (peers * CAPACITY, LANES), 0).astype(jnp.float32)
    picked = []
    for item in range(items):
        span = slice(item * rows, (item + 1) * rows)
        row = place[span, :].T[:1, :]
        pick = jnp.where(places == row, 1.0, 0.0).astype(jnp.bfloat16)
        picked.append(contract_matrices(pick, total[span, :], 1, 0))
    left = lax.broadcasted_iota(jnp.int32, (CAPACITY, LANES), 1) < LANES // 2
    lanes = pl.ds(pl.multiple_of(step * LANES, LANES), LANES)
    for w in range(peers):
        span = slice(w * CAPACITY, (w + 1) * CAPACITY)
        for half in range(2):
            pair = jnp.where(left, picked[half][span, :], picked[half + 2][span, :])
            first = rows + rank + half * CAPACITY
            out_ref[w, first : first + CAPACITY, lanes] = pair.astype(jnp.bfloat16)

    @pl.when(step == pl.num_programs(0) - 1)
    def _():
        for w in range(peers):
            out_ref[w, rows : rows + rank, :] = grad_ref[w * rank : (w + 1) * rank, :].astype(
                jnp.bfloat16
            )
        steps = peers // items
        tail = pl.ds(rows, rank + 2 * CAPACITY)
        rest = pltpu.make_async_copy(
            out_ref.at[:, tail, :], sent_ref.at[:, tail, :], sems.at[steps]
        )
        rest.start()
        for s in range(steps):
            done = pl.ds(s * items, items)
            pltpu.make_async_copy(
                out_ref.at[done, pl.ds(0, rows), :], sent_ref.at[done, pl.ds(0, rows), :], sems.at[s]
            ).wait()
        rest.wait()


def share_results(received, gathered, low, base, rows, rank):
    peer_count, _, share = received.shape
    keys = gathered.shape[2]
    block = STEP * rows
    slots = peer_count * rank
    total = rows + rank + 2 * CAPACITY
    once = pl.Buffered(1)
    return pl.pallas_call(
        share_kernel,
        grid=(peer_count // STEP,),
        in_specs=[
            pl.BlockSpec((STEP, rows, share), lambda s: (s, 0, 0)),
            pl.BlockSpec(
                (peer_count, rank, share), lambda s: (0, rows // rank, 0), pipeline_mode=once
            ),
            pl.BlockSpec(
                (STEP, INDEX_ROWS, keys), lambda s: (s, (rows + rank) // INDEX_ROWS, 0)
            ),
            pl.BlockSpec((block, LANES), lambda s: (s, 0)),
            pl.BlockSpec((block, share), lambda s: (s, 0)),
        ],
        out_specs=pl.BlockSpec(memory_space=pl.ANY),
        out_shape=jax.ShapeDtypeStruct((peer_count, total, share), jnp.bfloat16),
        scratch_shapes=[
            pltpu.VMEM((slots, share), jnp.float32),
            pltpu.VMEM((peer_count, total, share), jnp.bfloat16),
            pltpu.SemaphoreType.DMA((peer_count // STEP + 1,)),
        ],
        compiler_params=params(56),
        cost_estimate=pl.CostEstimate(flops=7 << 30, bytes_accessed=16 << 20, transcendentals=0),
    )(received, received, gathered, low, base)


def select_kernel(own_ref, cot_ref, place_ref, rows_ref, scale_ref):
    step = pl.program_id(0)
    items, rows, _ = cot_ref.shape
    place = place_columns(place_ref[...])
    first = own_ref[0] * CAPACITY
    wanted = first + lax.broadcasted_iota(jnp.int32, (CAPACITY, LANES), 0)
    wanted = wanted.astype(jnp.float32)

    @pl.when(step == 0)
    def _():
        scale_ref[...] = jnp.zeros_like(scale_ref)

    for item in range(items):
        row = place[item * rows : (item + 1) * rows, :].T[:1, :]
        pick = jnp.where(wanted == row, 1.0, 0.0)
        scale_ref[...] += jnp.sum(pick, axis=0, keepdims=True)
        chosen = contract_matrices(pick.astype(jnp.bfloat16), cot_ref[item], 1, 0)
        rows_ref[item * CAPACITY : (item + 1) * CAPACITY, :] = chosen.astype(jnp.bfloat16)

    @pl.when(step == pl.num_programs(0) - 1)
    def _():
        count = jnp.sum(scale_ref[...], axis=1, keepdims=True)
        scale_ref[...] = adapter_scale / jnp.maximum(jnp.broadcast_to(count, (1, LANES)), 1.0)


def select_rows(own, gathered, rows, rank):
    peer_count, _, keys = gathered.shape
    return pl.pallas_call(
        select_kernel,
        grid=(peer_count // STEP,),
        in_specs=[
            pl.BlockSpec(memory_space=pltpu.SMEM),
            pl.BlockSpec((STEP, rows, keys), lambda s: (s, 0, 0)),
            pl.BlockSpec(
                (STEP, INDEX_ROWS, keys), lambda s: (s, (rows + rank) // INDEX_ROWS, 0)
            ),
        ],
        out_specs=[
            pl.BlockSpec((STEP * CAPACITY, keys), lambda s: (s, 0)),
            pl.BlockSpec((1, LANES), lambda s: (0, 0)),
        ],
        out_shape=[
            jax.ShapeDtypeStruct((peer_count * CAPACITY, keys), jnp.bfloat16),
            jax.ShapeDtypeStruct((1, LANES), jnp.float32),
        ],
        compiler_params=params(56),
        cost_estimate=pl.CostEstimate(flops=1 << 29, bytes_accessed=8 << 20, transcendentals=0),
    )(own, gathered, gathered)


def finish_kernel(part_ref, cot_ref, scale_ref, grad_ref, gd_ref, gu_ref, acc):
    step = pl.program_id(0)
    items, _, share = part_ref.shape
    rows = grad_ref.shape[0]
    rank = gd_ref.shape[0]
    scale = scale_ref[...]

    @pl.when(step == 0)
    def _():
        acc[...] = jnp.zeros_like(acc)

    for item in range(items):
        span = slice(item * share, (item + 1) * share)
        grad_ref[:, span] = part_ref[item, :rows, :]
        gd_ref[:, span] = scale[0, 0] * part_ref[item, rows : rows + rank, :].astype(jnp.float32)
        acc[...] += part_ref[item, rows + rank :, :].astype(jnp.float32)

    @pl.when(step == pl.num_programs(0) - 1)
    def _():
        pieces = []
        for source in range(cot_ref.shape[0] // CAPACITY):
            chunk, half, first = source // 4, source % 4 // 2, source % 2 * CAPACITY
            piece = acc[first : first + CAPACITY, chunk * LANES : (chunk + 1) * LANES]
            pieces.append(pltpu.roll(piece, LANES // 2, 1) if half else piece)
        low = jnp.concatenate(pieces, axis=0).astype(jnp.bfloat16)
        gu_ref[...] = scale[0, 0] * contract_matrices(low, cot_ref[...], 0, 0)[:rank, :]


def finish(parts, chosen, scale, rows, rank):
    peer_count, total, share = parts.shape
    slots, keys = chosen.shape
    return pl.pallas_call(
        finish_kernel,
        grid=(peer_count // WIDE_STEP,),
        in_specs=[
            pl.BlockSpec((WIDE_STEP, total, share), lambda s: (s, 0, 0)),
            pl.BlockSpec((slots, keys), lambda s: (0, 0)),
            pl.BlockSpec((1, LANES), lambda s: (0, 0)),
        ],
        out_specs=[
            pl.BlockSpec((rows, WIDE_STEP * share), lambda s: (0, s)),
            pl.BlockSpec((rank, WIDE_STEP * share), lambda s: (0, s)),
            pl.BlockSpec((rank, keys), lambda s: (0, 0)),
        ],
        out_shape=[
            jax.ShapeDtypeStruct((rows, peer_count * share), jnp.bfloat16),
            jax.ShapeDtypeStruct((rank, peer_count * share), jnp.float32),
            jax.ShapeDtypeStruct((rank, keys), jnp.float32),
        ],
        scratch_shapes=[pltpu.VMEM((2 * CAPACITY, share), jnp.float32)],
        compiler_params=params(56),
        cost_estimate=pl.CostEstimate(flops=1 << 27, bytes_accessed=8 << 20, transcendentals=0),
    )(parts, chosen, scale)


def swap(block, mask):
    peer_count = lax.axis_size("wide")
    return lax.ppermute(block, "wide", [(i, i ^ mask) for i in range(peer_count)])


def spread(payload, packed):
    far, near, beside, core = 12, 4, 2, 1
    mirrored, packed = lax.optimization_barrier((swap(payload, far), packed))
    held = [(0, payload), (far, mirrored)]
    for mask in (near, beside, core):
        held = held + [(shift ^ mask, swap(block, mask)) for shift, block in held]
    for place in [4, 3, 6]:
        shift, block = held[place]
        packed, block = lax.optimization_barrier((packed, block))
        held[place] = (shift, block)
    return packed, held


def exchange(block):
    return lax.all_to_all(block, "wide", split_axis=0, concat_axis=0, tiled=True)


def column_body(
    features,
    cotangent,
    frozen_key_weight,
    adapter_down_weight,
    adapter_up_weight,
    row_adapter_index,
    device_adapter,
):
    rows = features.shape[0]
    rank = adapter_up_weight.shape[1]
    peer_count = lax.axis_size("wide")
    device_index = lax.axis_index("wide")
    payload = build_payload(
        cotangent, adapter_up_weight[0], row_adapter_index.reshape(1, rows), device_adapter
    )
    packed = pack_columns(features, adapter_down_weight[0].T, peer_count)
    packed, held = spread(payload, packed)
    received = exchange(packed)
    gathered = jnp.zeros((peer_count,) + payload.shape, payload.dtype)
    for shift, block in held:
        gathered = lax.dynamic_update_slice(gathered, block[None], (device_index ^ shift, 0, 0))
    low, base = low_out(gathered, frozen_key_weight, rows, rank)
    parts = exchange(share_results(received, gathered, low, base, rows, rank))
    own = jnp.full((1,), device_index, jnp.int32)
    chosen, scale = select_rows(own, gathered, rows, rank)
    input_grad, grad_down, grad_up = finish(parts, chosen, scale, rows, rank)
    return (input_grad, grad_down.T[None], grad_up[None])


def solution(mesh):
    in_specs = (
        P(("groups", "wide"), None),
        P(("groups", "wide"), None),
        P("wide", None),
        P(("groups", "wide"), None, None),
        P(("groups", "wide"), None, None),
        P(("groups", "wide"), None),
        P("groups"),
    )
    out_specs = (
        P(("groups", "wide"), None),
        P(("groups", "wide"), None, None),
        P(("groups", "wide"), None, None),
    )

    def body(*arrays):
        rows, width = arrays[0].shape
        keys = arrays[1].shape[1]
        rank = arrays[4].shape[1]
        peer_count = mesh.shape["wide"]
        by_columns = (
            peer_count == STEP * STEP
            and peer_count * rank <= keys
            and rank * 2 == LANES
            and rows == LANES
            and rows // INDEX_ROWS * LANES == keys
            and peer_count * rank == 2 * (width // peer_count)
        )
        return (column_body if by_columns else dispatch_body)(*arrays)

    return jax.shard_map(body, mesh=mesh, in_specs=in_specs, out_specs=out_specs, check_vma=False)
```

```python
import jax
import jax.numpy as jnp
from jax import lax
from jax.experimental import pallas as pl
from jax.experimental.pallas import tpu as pltpu
from jax.sharding import PartitionSpec as P

adapter_scale = 2.0
LANES = 128
INDEX_ROWS = 16
CAPACITY = 16
STEP = 4
WIDE_STEP = 8


def contract_matrices(left, right, left_dim, right_dim):
    return lax.dot_general(
        left, right, (((left_dim,), (right_dim,)), ((), ())), preferred_element_type=jnp.float32
    )


def frozen_part(cotangent, frozen_key_weight):
    return contract_matrices(
        cotangent, lax.all_gather(frozen_key_weight, "wide", axis=0, tiled=True), 1, 1
    )


def dispatch_body(
    features,
    cotangent,
    frozen_key_weight,
    adapter_down_weight,
    adapter_up_weight,
    row_adapter_index,
    device_adapter,
):
    row_count = features.shape[0]
    peer_count = lax.axis_size("wide")
    device_index = lax.axis_index("wide")
    capacity = max(2, 2 * row_count // peer_count)
    slot_range = jnp.arange(peer_count, dtype=jnp.int32)
    matches = row_adapter_index[:, 0][:, None] == device_adapter[None, :]
    token_slot = jnp.sum(jnp.where(matches, slot_range[None, :], 0), axis=1)
    slot_hit = (token_slot[:, None] == slot_range[None, :]).astype(jnp.int32)
    local_counts = jnp.sum(slot_hit, axis=0)
    token_counts = lax.psum(local_counts, "wide")
    earlier = jnp.cumsum(slot_hit, axis=0) - slot_hit
    token_rank = jnp.sum(earlier * slot_hit, axis=1)
    position = token_slot * capacity + token_rank
    slot_total = peer_count * capacity
    pick = position[None, :] == jnp.arange(slot_total, dtype=jnp.int32)[:, None]
    source_row = jnp.sum(
        jnp.where(pick, jnp.arange(row_count, dtype=jnp.int32)[None, :], 0), axis=1
    )
    filled = jnp.any(pick, axis=1)
    zero_value = jnp.zeros((), jnp.bfloat16)
    send_in = jnp.where(filled[:, None], features[source_row], zero_value).reshape(
        peer_count, capacity, -1
    )
    send_cot = jnp.where(filled[:, None], cotangent[source_row], zero_value).reshape(
        peer_count, capacity, -1
    )
    recv_in, recv_cot = (
        lax.all_to_all(send_in, "wide", split_axis=0, concat_axis=0, tiled=True),
        lax.all_to_all(send_cot, "wide", split_axis=0, concat_axis=0, tiled=True),
    )
    recv_in = recv_in.reshape(slot_total, -1)
    recv_cot = recv_cot.reshape(slot_total, -1)
    down_projection = adapter_down_weight[0]
    up_projection = adapter_up_weight[0]
    low_in = jnp.dot(recv_in, down_projection, preferred_element_type=jnp.float32).astype(
        jnp.bfloat16
    )
    low_rank_output = contract_matrices(recv_cot, up_projection, 1, 1).astype(jnp.bfloat16)
    rows_per_adapter = (
        adapter_scale * contract_matrices(low_rank_output, down_projection, 1, 1)
    ).astype(jnp.bfloat16)
    inverse_permutation = adapter_scale / jnp.maximum(token_counts[device_index], 1).astype(
        jnp.float32
    )
    grad_down = inverse_permutation * contract_matrices(recv_in, low_rank_output, 0, 0)
    grad_up = inverse_permutation * contract_matrices(low_in, recv_cot, 0, 0)
    returned = lax.all_to_all(
        rows_per_adapter.reshape(peer_count, capacity, -1),
        "wide",
        split_axis=0,
        concat_axis=0,
        tiled=True,
    )
    returned = returned.reshape(slot_total, -1)
    adapter_grad = returned[position]
    base_grad = frozen_part(cotangent, frozen_key_weight)
    input_grad = (base_grad + adapter_grad.astype(jnp.float32)).astype(jnp.bfloat16)
    return (input_grad, grad_down[None], grad_up[None])


def params(mebibytes):
    return pltpu.CompilerParams(vmem_limit_bytes=mebibytes * 1024 * 1024)


def place_columns(packed):
    values = packed.astype(jnp.float32)
    chunks = packed.shape[2] // LANES
    return jnp.concatenate(
        [
            values[item, :, j * LANES : (j + 1) * LANES]
            for item in range(packed.shape[0])
            for j in range(chunks)
        ],
        axis=0,
    )


def payload_kernel(cot_ref, up_ref, index_ref, adapters_ref, out_ref):
    rows = cot_ref.shape[0]
    rank = up_ref.shape[0]
    peers = adapters_ref.shape[0]
    out_ref[:rows, :] = cot_ref[...]
    out_ref[rows : rows + rank, :] = up_ref[...]
    index = index_ref[...]
    slot = jnp.zeros(index.shape, jnp.int32)
    for w in range(peers):
        slot = jnp.where(index == adapters_ref[w], w, slot)
    slot_range = lax.broadcasted_iota(jnp.int32, (peers, rows), 0)
    hits = jnp.where(slot_range == slot, 1.0, 0.0)
    before = lax.broadcasted_iota(jnp.int32, (rows, rows), 0)
    after = lax.broadcasted_iota(jnp.int32, (rows, rows), 1)
    earlier = jnp.where(before < after, 1.0, 0.0).astype(jnp.bfloat16)
    ranks = contract_matrices(hits.astype(jnp.bfloat16), earlier, 1, 0)
    order = jnp.sum(hits * ranks, axis=0, keepdims=True)
    place = slot.astype(jnp.float32) * CAPACITY + order
    marks = jnp.broadcast_to(place, (rows, rows)).T.astype(jnp.bfloat16)
    for j in range(rows // INDEX_ROWS):
        out_ref[rows + rank :, j * LANES : (j + 1) * LANES] = marks[
            j * INDEX_ROWS : (j + 1) * INDEX_ROWS, :
        ]


def build_payload(cotangent, up, index, adapters):
    total = cotangent.shape[0] + up.shape[0] + INDEX_ROWS
    vmem = pl.BlockSpec(memory_space=pltpu.VMEM)
    return pl.pallas_call(
        payload_kernel,
        in_specs=[vmem, vmem, vmem, pl.BlockSpec(memory_space=pltpu.SMEM)],
        out_shape=jax.ShapeDtypeStruct((total, cotangent.shape[1]), jnp.bfloat16),
        compiler_params=params(56),
        cost_estimate=pl.CostEstimate(flops=0, bytes_accessed=1 << 20, transcendentals=0),
    )(cotangent, up, index, adapters)


def pack_kernel(features_ref, down_ref, out_ref):
    rows = features_ref.shape[0]
    share = out_ref.shape[2]
    for d in range(out_ref.shape[0]):
        span = slice(d * share, (d + 1) * share)
        out_ref[d, :rows, :] = features_ref[:, span]
        out_ref[d, rows:, :] = down_ref[:, span]


def pack_columns(features, down, peer_count):
    rows, width = features.shape
    rank = down.shape[0]
    share = width // peer_count
    return pl.pallas_call(
        pack_kernel,
        grid=(peer_count // 2,),
        in_specs=[
            pl.BlockSpec((rows, 2 * share), lambda d: (0, d)),
            pl.BlockSpec((rank, 2 * share), lambda d: (0, d)),
        ],
        out_specs=pl.BlockSpec((2, rows + rank, share), lambda d: (d, 0, 0)),
        out_shape=jax.ShapeDtypeStruct((peer_count, rows + rank, share), jnp.bfloat16),
        compiler_params=params(56),
        cost_estimate=pl.CostEstimate(flops=0, bytes_accessed=6 << 20, transcendentals=0),
    )(features, down)


def adapter_lanes(j):
    lane = lax.broadcasted_iota(jnp.int32, (1, LANES), 1)
    return (2 * j + lane // (LANES // 2)).astype(jnp.float32)


def low_out_kernel(cot_ref, up_ref, place_ref, weight_ref, low_ref, base_ref):
    keys = cot_ref.shape[2]
    cot = cot_ref[...].reshape(-1, keys)
    slot = jnp.floor(place_columns(place_ref[...]) / CAPACITY)
    low = contract_matrices(cot, up_ref[...].reshape(-1, keys), 1, 1)
    total = jnp.zeros_like(slot)
    for j in range(low.shape[1] // LANES):
        span = slice(j * LANES, (j + 1) * LANES)
        total = total + jnp.where(slot == adapter_lanes(j), low[:, span], 0.0)
    low_ref[...] = (total + pltpu.roll(total, LANES // 2, 1)).astype(jnp.bfloat16)
    base_ref[...] = contract_matrices(cot, weight_ref[...], 1, 1)


def low_out(gathered, weight, rows, rank):
    peer_count, _, keys = gathered.shape
    share = weight.shape[0]
    block = STEP * rows
    once = pl.Buffered(1)
    return pl.pallas_call(
        low_out_kernel,
        grid=(peer_count // STEP,),
        in_specs=[
            pl.BlockSpec((STEP, rows, keys), lambda s: (s, 0, 0)),
            pl.BlockSpec(
                (peer_count, rank, keys), lambda s: (0, rows // rank, 0), pipeline_mode=once
            ),
            pl.BlockSpec(
                (STEP, INDEX_ROWS, keys), lambda s: (s, (rows + rank) // INDEX_ROWS, 0)
            ),
            pl.BlockSpec((share, keys), lambda s: (0, 0), pipeline_mode=once),
        ],
        out_specs=[
            pl.BlockSpec((block, LANES), lambda s: (s, 0)),
            pl.BlockSpec((block, share), lambda s: (s, 0)),
        ],
        out_shape=[
            jax.ShapeDtypeStruct((peer_count * rows, LANES), jnp.bfloat16),
            jax.ShapeDtypeStruct((peer_count * rows, share), jnp.float32),
        ],
        compiler_params=params(56),
        cost_estimate=pl.CostEstimate(flops=7 << 30, bytes_accessed=16 << 20, transcendentals=0),
    )(gathered, gathered, gathered, weight)


def share_kernel(feat_ref, down_ref, place_ref, low_ref, base_ref, sent_ref, grad_ref, out_ref, sems):
    step = pl.program_id(0)
    items, rows, share = feat_ref.shape
    peers, rank, _ = down_ref.shape

    @pl.when(step == 0)
    def _():
        grad_ref[...] = jnp.zeros_like(grad_ref)

    down = down_ref[...].reshape(-1, share)
    feat = feat_ref[...].reshape(-1, share)
    place = place_columns(place_ref[...])
    slot = jnp.floor(place / CAPACITY)
    folded = low_ref[...].astype(jnp.float32)
    masks = [slot == adapter_lanes(j) for j in range(down.shape[0] // LANES)]
    low = jnp.concatenate(
        [jnp.where(mine, folded, 0.0).astype(jnp.bfloat16) for mine in masks], axis=1
    )
    grad = base_ref[...] + adapter_scale * contract_matrices(low, down, 1, 0)
    block = pl.ds(step * items, items)
    out_ref[block, :rows, :] = grad.astype(jnp.bfloat16).reshape(items, rows, share)
    pltpu.make_async_copy(
        out_ref.at[block, pl.ds(0, rows), :], sent_ref.at[block, pl.ds(0, rows), :], sems.at[step]
    ).start()
    partial = contract_matrices(feat, down, 1, 1)
    grad_ref[...] += contract_matrices(low, feat, 0, 0)
    total = jnp.zeros_like(place)
    for j, mine in enumerate(masks):
        total = total + jnp.where(mine, partial[:, j * LANES : (j + 1) * LANES], 0.0)
    total = (total + pltpu.roll(total, LANES // 2, 1)).astype(jnp.bfloat16)
    places = lax.broadcasted_iota(jnp.int32, (peers * CAPACITY, LANES), 0).astype(jnp.float32)
    picked = []
    for item in range(items):
        span = slice(item * rows, (item + 1) * rows)
        row = place[span, :].T[:1, :]
        pick = jnp.where(places == row, 1.0, 0.0).astype(jnp.bfloat16)
        picked.append(contract_matrices(pick, total[span, :], 1, 0))
    left = lax.broadcasted_iota(jnp.int32, (CAPACITY, LANES), 1) < LANES // 2
    lanes = pl.ds(pl.multiple_of(step * LANES, LANES), LANES)
    for w in range(peers):
        span = slice(w * CAPACITY, (w + 1) * CAPACITY)
        for half in range(2):
            pair = jnp.where(left, picked[half][span, :], picked[half + 2][span, :])
            first = rows + rank + half * CAPACITY
            out_ref[w, first : first + CAPACITY, lanes] = pair.astype(jnp.bfloat16)

    @pl.when(step == pl.num_programs(0) - 1)
    def _():
        for w in range(peers):
            out_ref[w, rows : rows + rank, :] = grad_ref[w * rank : (w + 1) * rank, :].astype(
                jnp.bfloat16
            )
        steps = peers // items
        tail = pl.ds(rows, rank + 2 * CAPACITY)
        rest = pltpu.make_async_copy(
            out_ref.at[:, tail, :], sent_ref.at[:, tail, :], sems.at[steps]
        )
        rest.start()
        for s in range(steps):
            done = pl.ds(s * items, items)
            pltpu.make_async_copy(
                out_ref.at[done, pl.ds(0, rows), :], sent_ref.at[done, pl.ds(0, rows), :], sems.at[s]
            ).wait()
        rest.wait()


def share_results(received, gathered, low, base, rows, rank):
    peer_count, _, share = received.shape
    keys = gathered.shape[2]
    block = STEP * rows
    slots = peer_count * rank
    total = rows + rank + 2 * CAPACITY
    once = pl.Buffered(1)
    return pl.pallas_call(
        share_kernel,
        grid=(peer_count // STEP,),
        in_specs=[
            pl.BlockSpec((STEP, rows, share), lambda s: (s, 0, 0)),
            pl.BlockSpec(
                (peer_count, rank, share), lambda s: (0, rows // rank, 0), pipeline_mode=once
            ),
            pl.BlockSpec(
                (STEP, INDEX_ROWS, keys), lambda s: (s, (rows + rank) // INDEX_ROWS, 0)
            ),
            pl.BlockSpec((block, LANES), lambda s: (s, 0)),
            pl.BlockSpec((block, share), lambda s: (s, 0)),
        ],
        out_specs=pl.BlockSpec(memory_space=pl.ANY),
        out_shape=jax.ShapeDtypeStruct((peer_count, total, share), jnp.bfloat16),
        scratch_shapes=[
            pltpu.VMEM((slots, share), jnp.float32),
            pltpu.VMEM((peer_count, total, share), jnp.bfloat16),
            pltpu.SemaphoreType.DMA((peer_count // STEP + 1,)),
        ],
        compiler_params=params(56),
        cost_estimate=pl.CostEstimate(flops=7 << 30, bytes_accessed=16 << 20, transcendentals=0),
    )(received, received, gathered, low, base)


def select_kernel(own_ref, cot_ref, place_ref, rows_ref, scale_ref):
    step = pl.program_id(0)
    items, rows, _ = cot_ref.shape
    place = place_columns(place_ref[...])
    first = own_ref[0] * CAPACITY
    wanted = first + lax.broadcasted_iota(jnp.int32, (CAPACITY, LANES), 0)
    wanted = wanted.astype(jnp.float32)

    @pl.when(step == 0)
    def _():
        scale_ref[...] = jnp.zeros_like(scale_ref)

    for item in range(items):
        row = place[item * rows : (item + 1) * rows, :].T[:1, :]
        pick = jnp.where(wanted == row, 1.0, 0.0)
        scale_ref[...] += jnp.sum(pick, axis=0, keepdims=True)
        chosen = contract_matrices(pick.astype(jnp.bfloat16), cot_ref[item], 1, 0)
        rows_ref[item * CAPACITY : (item + 1) * CAPACITY, :] = chosen.astype(jnp.bfloat16)

    @pl.when(step == pl.num_programs(0) - 1)
    def _():
        count = jnp.sum(scale_ref[...], axis=1, keepdims=True)
        scale_ref[...] = adapter_scale / jnp.maximum(jnp.broadcast_to(count, (1, LANES)), 1.0)


def select_rows(own, gathered, rows, rank):
    peer_count, _, keys = gathered.shape
    return pl.pallas_call(
        select_kernel,
        grid=(peer_count // STEP,),
        in_specs=[
            pl.BlockSpec(memory_space=pltpu.SMEM),
            pl.BlockSpec((STEP, rows, keys), lambda s: (s, 0, 0)),
            pl.BlockSpec(
                (STEP, INDEX_ROWS, keys), lambda s: (s, (rows + rank) // INDEX_ROWS, 0)
            ),
        ],
        out_specs=[
            pl.BlockSpec((STEP * CAPACITY, keys), lambda s: (s, 0)),
            pl.BlockSpec((1, LANES), lambda s: (0, 0)),
        ],
        out_shape=[
            jax.ShapeDtypeStruct((peer_count * CAPACITY, keys), jnp.bfloat16),
            jax.ShapeDtypeStruct((1, LANES), jnp.float32),
        ],
        compiler_params=params(44),
        cost_estimate=pl.CostEstimate(flops=1 << 29, bytes_accessed=8 << 20, transcendentals=0),
    )(own, gathered, gathered)


def finish_kernel(part_ref, cot_ref, scale_ref, grad_ref, gd_ref, gu_ref, acc):
    step = pl.program_id(0)
    items, _, share = part_ref.shape
    rows = grad_ref.shape[0]
    rank = gd_ref.shape[0]
    scale = scale_ref[...]

    @pl.when(step == 0)
    def _():
        acc[...] = jnp.zeros_like(acc)

    for item in range(items):
        span = slice(item * share, (item + 1) * share)
        grad_ref[:, span] = part_ref[item, :rows, :]
        gd_ref[:, span] = scale[0, 0] * part_ref[item, rows : rows + rank, :].astype(jnp.float32)
        acc[...] += part_ref[item, rows + rank :, :].astype(jnp.float32)

    @pl.when(step == pl.num_programs(0) - 1)
    def _():
        pieces = []
        for source in range(cot_ref.shape[0] // CAPACITY):
            chunk, half, first = source // 4, source % 4 // 2, source % 2 * CAPACITY
            piece = acc[first : first + CAPACITY, chunk * LANES : (chunk + 1) * LANES]
            pieces.append(pltpu.roll(piece, LANES // 2, 1) if half else piece)
        low = jnp.concatenate(pieces, axis=0).astype(jnp.bfloat16)
        gu_ref[...] = scale[0, 0] * contract_matrices(low, cot_ref[...], 0, 0)[:rank, :]


def finish(parts, chosen, scale, rows, rank):
    peer_count, total, share = parts.shape
    slots, keys = chosen.shape
    return pl.pallas_call(
        finish_kernel,
        grid=(peer_count // WIDE_STEP,),
        in_specs=[
            pl.BlockSpec((WIDE_STEP, total, share), lambda s: (s, 0, 0)),
            pl.BlockSpec((slots, keys), lambda s: (0, 0)),
            pl.BlockSpec((1, LANES), lambda s: (0, 0)),
        ],
        out_specs=[
            pl.BlockSpec((rows, WIDE_STEP * share), lambda s: (0, s)),
            pl.BlockSpec((rank, WIDE_STEP * share), lambda s: (0, s)),
            pl.BlockSpec((rank, keys), lambda s: (0, 0)),
        ],
        out_shape=[
            jax.ShapeDtypeStruct((rows, peer_count * share), jnp.bfloat16),
            jax.ShapeDtypeStruct((rank, peer_count * share), jnp.float32),
            jax.ShapeDtypeStruct((rank, keys), jnp.float32),
        ],
        scratch_shapes=[pltpu.VMEM((2 * CAPACITY, share), jnp.float32)],
        compiler_params=params(44),
        cost_estimate=pl.CostEstimate(flops=1 << 27, bytes_accessed=8 << 20, transcendentals=0),
    )(parts, chosen, scale)


def swap(block, mask):
    peer_count = lax.axis_size("wide")
    return lax.ppermute(block, "wide", [(i, i ^ mask) for i in range(peer_count)])


def spread(payload, packed):
    far, near, beside, core = 12, 4, 2, 1
    mirrored, packed = lax.optimization_barrier((swap(payload, far), packed))
    held = [(0, payload), (far, mirrored)]
    for mask in (near, beside, core):
        held = held + [(shift ^ mask, swap(block, mask)) for shift, block in held]
    for place in [4, 3, 6]:
        shift, block = held[place]
        packed, block = lax.optimization_barrier((packed, block))
        held[place] = (shift, block)
    late = [5, 7, 13, 15]
    return packed, [held[i] for i in range(16) if i not in late] + [held[i] for i in late]


def exchange(block):
    return lax.all_to_all(block, "wide", split_axis=0, concat_axis=0, tiled=True)


def column_body(
    features,
    cotangent,
    frozen_key_weight,
    adapter_down_weight,
    adapter_up_weight,
    row_adapter_index,
    device_adapter,
):
    rows = features.shape[0]
    rank = adapter_up_weight.shape[1]
    peer_count = lax.axis_size("wide")
    device_index = lax.axis_index("wide")
    payload = build_payload(
        cotangent, adapter_up_weight[0], row_adapter_index.reshape(1, rows), device_adapter
    )
    packed = pack_columns(features, adapter_down_weight[0].T, peer_count)
    packed, held = spread(payload, packed)
    received = exchange(packed)
    gathered = jnp.zeros((peer_count,) + payload.shape, payload.dtype)
    for shift, block in held:
        gathered = lax.dynamic_update_slice(gathered, block[None], (device_index ^ shift, 0, 0))
    low, base = low_out(gathered, frozen_key_weight, rows, rank)
    parts = exchange(share_results(received, gathered, low, base, rows, rank))
    own = jnp.full((1,), device_index, jnp.int32)
    chosen, scale = select_rows(own, gathered, rows, rank)
    input_grad, grad_down, grad_up = finish(parts, chosen, scale, rows, rank)
    return (input_grad, grad_down.T[None], grad_up[None])


def solution(mesh):
    in_specs = (
        P(("groups", "wide"), None),
        P(("groups", "wide"), None),
        P("wide", None),
        P(("groups", "wide"), None, None),
        P(("groups", "wide"), None, None),
        P(("groups", "wide"), None),
        P("groups"),
    )
    out_specs = (
        P(("groups", "wide"), None),
        P(("groups", "wide"), None, None),
        P(("groups", "wide"), None, None),
    )

    def body(*arrays):
        rows, width = arrays[0].shape
        keys = arrays[1].shape[1]
        rank = arrays[4].shape[1]
        peer_count = mesh.shape["wide"]
        by_columns = (
            peer_count == STEP * STEP
            and peer_count * rank <= keys
            and rank * 2 == LANES
            and rows == LANES
            and rows // INDEX_ROWS * LANES == keys
            and peer_count * rank == 2 * (width // peer_count)
        )
        return (column_body if by_columns else dispatch_body)(*arrays)

    return jax.shard_map(body, mesh=mesh, in_specs=in_specs, out_specs=out_specs, check_vma=False)
```

```python
import jax
import jax.numpy as jnp
from jax import lax
from jax.experimental import pallas as pl
from jax.experimental.pallas import tpu as pltpu
from jax.sharding import PartitionSpec as P

adapter_scale = 2.0
LANES = 128
INDEX_ROWS = 16
CAPACITY = 16
STEP = 4
WIDE_STEP = 8


def contract_matrices(left, right, left_dim, right_dim):
    return lax.dot_general(
        left, right, (((left_dim,), (right_dim,)), ((), ())), preferred_element_type=jnp.float32
    )


def frozen_part(cotangent, frozen_key_weight):
    return contract_matrices(
        cotangent, lax.all_gather(frozen_key_weight, "wide", axis=0, tiled=True), 1, 1
    )


def dispatch_body(
    features,
    cotangent,
    frozen_key_weight,
    adapter_down_weight,
    adapter_up_weight,
    row_adapter_index,
    device_adapter,
):
    row_count = features.shape[0]
    peer_count = lax.axis_size("wide")
    device_index = lax.axis_index("wide")
    capacity = max(2, 2 * row_count // peer_count)
    slot_range = jnp.arange(peer_count, dtype=jnp.int32)
    matches = row_adapter_index[:, 0][:, None] == device_adapter[None, :]
    token_slot = jnp.sum(jnp.where(matches, slot_range[None, :], 0), axis=1)
    slot_hit = (token_slot[:, None] == slot_range[None, :]).astype(jnp.int32)
    local_counts = jnp.sum(slot_hit, axis=0)
    token_counts = lax.psum(local_counts, "wide")
    earlier = jnp.cumsum(slot_hit, axis=0) - slot_hit
    token_rank = jnp.sum(earlier * slot_hit, axis=1)
    position = token_slot * capacity + token_rank
    slot_total = peer_count * capacity
    pick = position[None, :] == jnp.arange(slot_total, dtype=jnp.int32)[:, None]
    source_row = jnp.sum(
        jnp.where(pick, jnp.arange(row_count, dtype=jnp.int32)[None, :], 0), axis=1
    )
    filled = jnp.any(pick, axis=1)
    zero_value = jnp.zeros((), jnp.bfloat16)
    send_in = jnp.where(filled[:, None], features[source_row], zero_value).reshape(
        peer_count, capacity, -1
    )
    send_cot = jnp.where(filled[:, None], cotangent[source_row], zero_value).reshape(
        peer_count, capacity, -1
    )
    recv_in, recv_cot = (
        lax.all_to_all(send_in, "wide", split_axis=0, concat_axis=0, tiled=True),
        lax.all_to_all(send_cot, "wide", split_axis=0, concat_axis=0, tiled=True),
    )
    recv_in = recv_in.reshape(slot_total, -1)
    recv_cot = recv_cot.reshape(slot_total, -1)
    down_projection = adapter_down_weight[0]
    up_projection = adapter_up_weight[0]
    low_in = jnp.dot(recv_in, down_projection, preferred_element_type=jnp.float32).astype(
        jnp.bfloat16
    )
    low_rank_output = contract_matrices(recv_cot, up_projection, 1, 1).astype(jnp.bfloat16)
    rows_per_adapter = (
        adapter_scale * contract_matrices(low_rank_output, down_projection, 1, 1)
    ).astype(jnp.bfloat16)
    inverse_permutation = adapter_scale / jnp.maximum(token_counts[device_index], 1).astype(
        jnp.float32
    )
    grad_down = inverse_permutation * contract_matrices(recv_in, low_rank_output, 0, 0)
    grad_up = inverse_permutation * contract_matrices(low_in, recv_cot, 0, 0)
    returned = lax.all_to_all(
        rows_per_adapter.reshape(peer_count, capacity, -1),
        "wide",
        split_axis=0,
        concat_axis=0,
        tiled=True,
    )
    returned = returned.reshape(slot_total, -1)
    adapter_grad = returned[position]
    base_grad = frozen_part(cotangent, frozen_key_weight)
    input_grad = (base_grad + adapter_grad.astype(jnp.float32)).astype(jnp.bfloat16)
    return (input_grad, grad_down[None], grad_up[None])


def params(mebibytes):
    return pltpu.CompilerParams(vmem_limit_bytes=mebibytes * 1024 * 1024)


def place_columns(packed):
    values = packed.astype(jnp.float32)
    chunks = packed.shape[2] // LANES
    return jnp.concatenate(
        [
            values[item, :, j * LANES : (j + 1) * LANES]
            for item in range(packed.shape[0])
            for j in range(chunks)
        ],
        axis=0,
    )


def payload_kernel(cot_ref, up_ref, index_ref, adapters_ref, out_ref):
    rows = cot_ref.shape[0]
    rank = up_ref.shape[0]
    peers = adapters_ref.shape[0]
    out_ref[:rows, :] = cot_ref[...]
    out_ref[rows : rows + rank, :] = up_ref[...]
    index = index_ref[...]
    slot = jnp.zeros(index.shape, jnp.int32)
    for w in range(peers):
        slot = jnp.where(index == adapters_ref[w], w, slot)
    slot_range = lax.broadcasted_iota(jnp.int32, (peers, rows), 0)
    hits = jnp.where(slot_range == slot, 1.0, 0.0)
    before = lax.broadcasted_iota(jnp.int32, (rows, rows), 0)
    after = lax.broadcasted_iota(jnp.int32, (rows, rows), 1)
    earlier = jnp.where(before < after, 1.0, 0.0).astype(jnp.bfloat16)
    ranks = contract_matrices(hits.astype(jnp.bfloat16), earlier, 1, 0)
    order = jnp.sum(hits * ranks, axis=0, keepdims=True)
    place = slot.astype(jnp.float32) * CAPACITY + order
    marks = jnp.broadcast_to(place, (rows, rows)).T.astype(jnp.bfloat16)
    for j in range(rows // INDEX_ROWS):
        out_ref[rows + rank :, j * LANES : (j + 1) * LANES] = marks[
            j * INDEX_ROWS : (j + 1) * INDEX_ROWS, :
        ]


def build_payload(cotangent, up, index, adapters):
    total = cotangent.shape[0] + up.shape[0] + INDEX_ROWS
    vmem = pl.BlockSpec(memory_space=pltpu.VMEM)
    return pl.pallas_call(
        payload_kernel,
        in_specs=[vmem, vmem, vmem, pl.BlockSpec(memory_space=pltpu.SMEM)],
        out_shape=jax.ShapeDtypeStruct((total, cotangent.shape[1]), jnp.bfloat16),
        compiler_params=params(56),
        cost_estimate=pl.CostEstimate(flops=0, bytes_accessed=1 << 20, transcendentals=0),
    )(cotangent, up, index, adapters)


def pack_kernel(features_ref, down_ref, out_ref):
    rows = features_ref.shape[0]
    share = out_ref.shape[2]
    for d in range(out_ref.shape[0]):
        span = slice(d * share, (d + 1) * share)
        out_ref[d, :rows, :] = features_ref[:, span]
        out_ref[d, rows:, :] = down_ref[:, span]


def pack_columns(features, down, peer_count):
    rows, width = features.shape
    rank = down.shape[0]
    share = width // peer_count
    return pl.pallas_call(
        pack_kernel,
        grid=(peer_count // 2,),
        in_specs=[
            pl.BlockSpec((rows, 2 * share), lambda d: (0, d)),
            pl.BlockSpec((rank, 2 * share), lambda d: (0, d)),
        ],
        out_specs=pl.BlockSpec((2, rows + rank, share), lambda d: (d, 0, 0)),
        out_shape=jax.ShapeDtypeStruct((peer_count, rows + rank, share), jnp.bfloat16),
        compiler_params=params(56),
        cost_estimate=pl.CostEstimate(flops=0, bytes_accessed=6 << 20, transcendentals=0),
    )(features, down)


def adapter_lanes(j):
    lane = lax.broadcasted_iota(jnp.int32, (1, LANES), 1)
    return (2 * j + lane // (LANES // 2)).astype(jnp.float32)


def low_out_kernel(cot_ref, up_ref, place_ref, weight_ref, low_ref, base_ref, pick_ref):
    keys = cot_ref.shape[2]
    cot = cot_ref[...].reshape(-1, keys)
    slot = jnp.floor(place_columns(place_ref[...]) / CAPACITY)
    low = contract_matrices(cot, up_ref[...].reshape(-1, keys), 1, 1)
    total = jnp.zeros_like(slot)
    for j in range(low.shape[1] // LANES):
        span = slice(j * LANES, (j + 1) * LANES)
        total = total + jnp.where(slot == adapter_lanes(j), low[:, span], 0.0)
    low_ref[...] = (total + pltpu.roll(total, LANES // 2, 1)).astype(jnp.bfloat16)
    base_ref[...] = contract_matrices(cot, weight_ref[...], 1, 1)
    items, places, rows = pick_ref.shape
    place = place_columns(place_ref[...])
    wanted = lax.broadcasted_iota(jnp.int32, (places, rows), 0).astype(jnp.float32)
    for item in range(items):
        row = place[item * rows : (item + 1) * rows, :].T[:1, :]
        pick_ref[item] = jnp.where(wanted == row, 1.0, 0.0).astype(jnp.bfloat16)


def low_out(gathered, weight, rows, rank):
    peer_count, _, keys = gathered.shape
    share = weight.shape[0]
    block = STEP * rows
    once = pl.Buffered(1)
    return pl.pallas_call(
        low_out_kernel,
        grid=(peer_count // STEP,),
        in_specs=[
            pl.BlockSpec((STEP, rows, keys), lambda s: (s, 0, 0)),
            pl.BlockSpec(
                (peer_count, rank, keys), lambda s: (0, rows // rank, 0), pipeline_mode=once
            ),
            pl.BlockSpec(
                (STEP, INDEX_ROWS, keys), lambda s: (s, (rows + rank) // INDEX_ROWS, 0)
            ),
            pl.BlockSpec((share, keys), lambda s: (0, 0), pipeline_mode=once),
        ],
        out_specs=[
            pl.BlockSpec((block, LANES), lambda s: (s, 0)),
            pl.BlockSpec((block, share), lambda s: (s, 0)),
            pl.BlockSpec((STEP, peer_count * CAPACITY, rows), lambda s: (s, 0, 0)),
        ],
        out_shape=[
            jax.ShapeDtypeStruct((peer_count * rows, LANES), jnp.bfloat16),
            jax.ShapeDtypeStruct((peer_count * rows, share), jnp.float32),
            jax.ShapeDtypeStruct((peer_count, peer_count * CAPACITY, rows), jnp.bfloat16),
        ],
        compiler_params=params(56),
        cost_estimate=pl.CostEstimate(flops=7 << 30, bytes_accessed=16 << 20, transcendentals=0),
    )(gathered, gathered, gathered, weight)


def share_kernel(feat_ref, down_ref, place_ref, low_ref, base_ref, pick_ref, sent_ref, grad_ref, out_ref, sems):
    step = pl.program_id(0)
    items, rows, share = feat_ref.shape
    peers, rank, _ = down_ref.shape

    @pl.when(step == 0)
    def _():
        grad_ref[...] = jnp.zeros_like(grad_ref)

    down = down_ref[...].reshape(-1, share)
    feat = feat_ref[...].reshape(-1, share)
    place = place_columns(place_ref[...])
    slot = jnp.floor(place / CAPACITY)
    folded = low_ref[...].astype(jnp.float32)
    masks = [slot == adapter_lanes(j) for j in range(down.shape[0] // LANES)]
    low = jnp.concatenate(
        [jnp.where(mine, folded, 0.0).astype(jnp.bfloat16) for mine in masks], axis=1
    )
    grad = base_ref[...] + adapter_scale * contract_matrices(low, down, 1, 0)
    block = pl.ds(step * items, items)
    out_ref[block, :rows, :] = grad.astype(jnp.bfloat16).reshape(items, rows, share)
    pltpu.make_async_copy(
        out_ref.at[block, pl.ds(0, rows), :], sent_ref.at[block, pl.ds(0, rows), :], sems.at[step]
    ).start()
    partial = contract_matrices(feat, down, 1, 1)
    grad_ref[...] += contract_matrices(low, feat, 0, 0)
    total = jnp.zeros_like(place)
    for j, mine in enumerate(masks):
        total = total + jnp.where(mine, partial[:, j * LANES : (j + 1) * LANES], 0.0)
    total = (total + pltpu.roll(total, LANES // 2, 1)).astype(jnp.bfloat16)
    picked = []
    for item in range(items):
        span = slice(item * rows, (item + 1) * rows)
        picked.append(contract_matrices(pick_ref[item], total[span, :], 1, 0))
    left = lax.broadcasted_iota(jnp.int32, (CAPACITY, LANES), 1) < LANES // 2
    lanes = pl.ds(pl.multiple_of(step * LANES, LANES), LANES)
    for w in range(peers):
        span = slice(w * CAPACITY, (w + 1) * CAPACITY)
        for half in range(2):
            pair = jnp.where(left, picked[half][span, :], picked[half + 2][span, :])
            first = rows + rank + half * CAPACITY
            out_ref[w, first : first + CAPACITY, lanes] = pair.astype(jnp.bfloat16)

    @pl.when(step == pl.num_programs(0) - 1)
    def _():
        for w in range(peers):
            out_ref[w, rows : rows + rank, :] = grad_ref[w * rank : (w + 1) * rank, :].astype(
                jnp.bfloat16
            )
        steps = peers // items
        tail = pl.ds(rows, rank + 2 * CAPACITY)
        rest = pltpu.make_async_copy(
            out_ref.at[:, tail, :], sent_ref.at[:, tail, :], sems.at[steps]
        )
        rest.start()
        for s in range(steps):
            done = pl.ds(s * items, items)
            pltpu.make_async_copy(
                out_ref.at[done, pl.ds(0, rows), :], sent_ref.at[done, pl.ds(0, rows), :], sems.at[s]
            ).wait()
        rest.wait()


def share_results(received, gathered, low, base, picks, rows, rank):
    peer_count, _, share = received.shape
    keys = gathered.shape[2]
    block = STEP * rows
    slots = peer_count * rank
    total = rows + rank + 2 * CAPACITY
    once = pl.Buffered(1)
    return pl.pallas_call(
        share_kernel,
        grid=(peer_count // STEP,),
        in_specs=[
            pl.BlockSpec((STEP, rows, share), lambda s: (s, 0, 0)),
            pl.BlockSpec(
                (peer_count, rank, share), lambda s: (0, rows // rank, 0), pipeline_mode=once
            ),
            pl.BlockSpec(
                (STEP, INDEX_ROWS, keys), lambda s: (s, (rows + rank) // INDEX_ROWS, 0)
            ),
            pl.BlockSpec((block, LANES), lambda s: (s, 0)),
            pl.BlockSpec((block, share), lambda s: (s, 0)),
            pl.BlockSpec((STEP, peer_count * CAPACITY, rows), lambda s: (s, 0, 0)),
        ],
        out_specs=pl.BlockSpec(memory_space=pl.ANY),
        out_shape=jax.ShapeDtypeStruct((peer_count, total, share), jnp.bfloat16),
        scratch_shapes=[
            pltpu.VMEM((slots, share), jnp.float32),
            pltpu.VMEM((peer_count, total, share), jnp.bfloat16),
            pltpu.SemaphoreType.DMA((peer_count // STEP + 1,)),
        ],
        compiler_params=params(56),
        cost_estimate=pl.CostEstimate(flops=7 << 30, bytes_accessed=16 << 20, transcendentals=0),
    )(received, received, gathered, low, base, picks)


def select_kernel(own_ref, cot_ref, place_ref, rows_ref, scale_ref):
    step = pl.program_id(0)
    items, rows, _ = cot_ref.shape
    place = place_columns(place_ref[...])
    first = own_ref[0] * CAPACITY
    wanted = first + lax.broadcasted_iota(jnp.int32, (CAPACITY, LANES), 0)
    wanted = wanted.astype(jnp.float32)

    @pl.when(step == 0)
    def _():
        scale_ref[...] = jnp.zeros_like(scale_ref)

    for item in range(items):
        row = place[item * rows : (item + 1) * rows, :].T[:1, :]
        pick = jnp.where(wanted == row, 1.0, 0.0)
        scale_ref[...] += jnp.sum(pick, axis=0, keepdims=True)
        chosen = contract_matrices(pick.astype(jnp.bfloat16), cot_ref[item], 1, 0)
        rows_ref[item * CAPACITY : (item + 1) * CAPACITY, :] = chosen.astype(jnp.bfloat16)

    @pl.when(step == pl.num_programs(0) - 1)
    def _():
        count = jnp.sum(scale_ref[...], axis=1, keepdims=True)
        scale_ref[...] = adapter_scale / jnp.maximum(jnp.broadcast_to(count, (1, LANES)), 1.0)


def select_rows(own, gathered, rows, rank):
    peer_count, _, keys = gathered.shape
    return pl.pallas_call(
        select_kernel,
        grid=(peer_count // STEP,),
        in_specs=[
            pl.BlockSpec(memory_space=pltpu.SMEM),
            pl.BlockSpec((STEP, rows, keys), lambda s: (s, 0, 0)),
            pl.BlockSpec(
                (STEP, INDEX_ROWS, keys), lambda s: (s, (rows + rank) // INDEX_ROWS, 0)
            ),
        ],
        out_specs=[
            pl.BlockSpec((STEP * CAPACITY, keys), lambda s: (s, 0)),
            pl.BlockSpec((1, LANES), lambda s: (0, 0)),
        ],
        out_shape=[
            jax.ShapeDtypeStruct((peer_count * CAPACITY, keys), jnp.bfloat16),
            jax.ShapeDtypeStruct((1, LANES), jnp.float32),
        ],
        compiler_params=params(44),
        cost_estimate=pl.CostEstimate(flops=1 << 29, bytes_accessed=8 << 20, transcendentals=0),
    )(own, gathered, gathered)


def finish_kernel(part_ref, cot_ref, scale_ref, grad_ref, gd_ref, gu_ref, acc):
    step = pl.program_id(0)
    items, _, share = part_ref.shape
    rows = grad_ref.shape[0]
    rank = gd_ref.shape[0]
    scale = scale_ref[...]

    @pl.when(step == 0)
    def _():
        acc[...] = jnp.zeros_like(acc)

    for item in range(items):
        span = slice(item * share, (item + 1) * share)
        grad_ref[:, span] = part_ref[item, :rows, :]
        gd_ref[:, span] = scale[0, 0] * part_ref[item, rows : rows + rank, :].astype(jnp.float32)
        acc[...] += part_ref[item, rows + rank :, :].astype(jnp.float32)

    @pl.when(step == pl.num_programs(0) - 1)
    def _():
        pieces = []
        for source in range(cot_ref.shape[0] // CAPACITY):
            chunk, half, first = source // 4, source % 4 // 2, source % 2 * CAPACITY
            piece = acc[first : first + CAPACITY, chunk * LANES : (chunk + 1) * LANES]
            pieces.append(pltpu.roll(piece, LANES // 2, 1) if half else piece)
        low = jnp.concatenate(pieces, axis=0).astype(jnp.bfloat16)
        gu_ref[...] = scale[0, 0] * contract_matrices(low, cot_ref[...], 0, 0)[:rank, :]


def finish(parts, chosen, scale, rows, rank):
    peer_count, total, share = parts.shape
    slots, keys = chosen.shape
    return pl.pallas_call(
        finish_kernel,
        grid=(peer_count // WIDE_STEP,),
        in_specs=[
            pl.BlockSpec((WIDE_STEP, total, share), lambda s: (s, 0, 0)),
            pl.BlockSpec((slots, keys), lambda s: (0, 0)),
            pl.BlockSpec((1, LANES), lambda s: (0, 0)),
        ],
        out_specs=[
            pl.BlockSpec((rows, WIDE_STEP * share), lambda s: (0, s)),
            pl.BlockSpec((rank, WIDE_STEP * share), lambda s: (0, s)),
            pl.BlockSpec((rank, keys), lambda s: (0, 0)),
        ],
        out_shape=[
            jax.ShapeDtypeStruct((rows, peer_count * share), jnp.bfloat16),
            jax.ShapeDtypeStruct((rank, peer_count * share), jnp.float32),
            jax.ShapeDtypeStruct((rank, keys), jnp.float32),
        ],
        scratch_shapes=[pltpu.VMEM((2 * CAPACITY, share), jnp.float32)],
        compiler_params=params(44),
        cost_estimate=pl.CostEstimate(flops=1 << 27, bytes_accessed=8 << 20, transcendentals=0),
    )(parts, chosen, scale)


def swap(block, mask):
    peer_count = lax.axis_size("wide")
    return lax.ppermute(block, "wide", [(i, i ^ mask) for i in range(peer_count)])


def spread(payload, packed):
    far, near, beside, core = 12, 4, 2, 1
    mirrored, packed = lax.optimization_barrier((swap(payload, far), packed))
    held = [(0, payload), (far, mirrored)]
    for mask in (near, beside, core):
        held = held + [(shift ^ mask, swap(block, mask)) for shift, block in held]
    for place in [4, 3, 6]:
        shift, block = held[place]
        packed, block = lax.optimization_barrier((packed, block))
        held[place] = (shift, block)
    late = [5, 7, 13, 15]
    return packed, [held[i] for i in range(16) if i not in late] + [held[i] for i in late]


def exchange(block):
    return lax.all_to_all(block, "wide", split_axis=0, concat_axis=0, tiled=True)


def column_body(
    features,
    cotangent,
    frozen_key_weight,
    adapter_down_weight,
    adapter_up_weight,
    row_adapter_index,
    device_adapter,
):
    rows = features.shape[0]
    rank = adapter_up_weight.shape[1]
    peer_count = lax.axis_size("wide")
    device_index = lax.axis_index("wide")
    payload = build_payload(
        cotangent, adapter_up_weight[0], row_adapter_index.reshape(1, rows), device_adapter
    )
    packed = pack_columns(features, adapter_down_weight[0].T, peer_count)
    packed, held = spread(payload, packed)
    received = exchange(packed)
    gathered = jnp.zeros((peer_count,) + payload.shape, payload.dtype)
    for shift, block in held:
        gathered = lax.dynamic_update_slice(gathered, block[None], (device_index ^ shift, 0, 0))
    low, base, picks = low_out(gathered, frozen_key_weight, rows, rank)
    parts = exchange(share_results(received, gathered, low, base, picks, rows, rank))
    own = jnp.full((1,), device_index, jnp.int32)
    chosen, scale = select_rows(own, gathered, rows, rank)
    input_grad, grad_down, grad_up = finish(parts, chosen, scale, rows, rank)
    return (input_grad, grad_down.T[None], grad_up[None])


def solution(mesh):
    in_specs = (
        P(("groups", "wide"), None),
        P(("groups", "wide"), None),
        P("wide", None),
        P(("groups", "wide"), None, None),
        P(("groups", "wide"), None, None),
        P(("groups", "wide"), None),
        P("groups"),
    )
    out_specs = (
        P(("groups", "wide"), None),
        P(("groups", "wide"), None, None),
        P(("groups", "wide"), None, None),
    )

    def body(*arrays):
        rows, width = arrays[0].shape
        keys = arrays[1].shape[1]
        rank = arrays[4].shape[1]
        peer_count = mesh.shape["wide"]
        by_columns = (
            peer_count == STEP * STEP
            and peer_count * rank <= keys
            and rank * 2 == LANES
            and rows == LANES
            and rows // INDEX_ROWS * LANES == keys
            and peer_count * rank == 2 * (width // peer_count)
        )
        return (column_body if by_columns else dispatch_body)(*arrays)

    return jax.shard_map(body, mesh=mesh, in_specs=in_specs, out_specs=out_specs, check_vma=False)
```
